32 devices in a mesh: space: 8 (over z, x), chan: 4 (over y, core).
Axes of the slice: x: 2, y: 2, z: 4, core: 2. Of those that a mesh axis runs over, the one named last changes fastest.
Arguments:
- features: float32 [256, 4096], P('chan', 'space'), may hold values from -6 to 6
- positions: float32 [3, 4096], P(None, 'space'), may hold values from 0 to 2, as said below
- counts: int32 [16], P('space'), may hold values from 1 to 256, as said below
- neighbours: int32 [16, 4], P('space'), may hold values from 0 to 5, as said below
- wavevectors: int32 [3, 512], replicated, may hold values from -4 to 4, as said below
- filters: float32 [8, 256, 256], P(None, 'chan'), may hold values from -0.125 to 0.125
- cotangent: float32 [256, 4096], P('chan', 'space'), may hold values from -6 to 6
Outputs:
- updated: float32 [256, 4096], P('chan', 'space')
- grad_features: float32 [256, 4096], P('chan', 'space')
The draws below stay inside these ranges and needn't reach their ends.
Inputs may be any that keep to these rules, and one draw needn't show every extreme that they name: `counts`: at least one block holds 256 live atoms. `neighbours`: entry e names block e mod 2 of the previous (e // 2 = 0), the same (1) or the next (2) slab layer, the layers closing into a loop; the first entry of a row is the block itself, the entries of a row differ, and each names a block whose position within its layer differs from the row's by at most one. `wavevectors`: no column is all zeros. `positions`: the first coordinate lies in [0, 1], the second in [b, b + 1] for the b-th block of a layer, the third in [0, 1].
All inputs are finite; a program needn't handle non-finite values.
Results may differ from the reference program's by a relative error of at most 0.0003.
Values sent between devices are 32-bit elements; how exact they have to be, the bound alone decides.
A program may use at most 64 MiB of HBM per device.

```python
import math
import jax
import jax.numpy as jnp
from jax import lax

C = 256
NRAD = 8
K = 512
NB = 4
CAP = 256
BLK_DEV = 2
BLOCKS = 16
SLOTS = 4096
N_SPACE = 8


def draw_positions(key, part):
    unit = jax.random.uniform(key, (3, SLOTS), jnp.float32)
    slot_index = jnp.arange(SLOTS)
    local_block = (slot_index // CAP % BLK_DEV).astype(jnp.float32)
    return jnp.stack([unit[0], local_block + unit[1], unit[2]]).astype(jnp.float32)


def draw_counts(key, part):
    first_key, second_key, third_key = jax.random.split(jax.random.fold_in(key, 11), 3)
    one_draw = jax.random.randint(first_key, (BLOCKS,), 1, CAP + 1)
    two_draw = jax.random.randint(second_key, (BLOCKS,), 1, CAP + 1)
    fuller = jax.random.randint(third_key, (), 0, BLOCKS)
    return jnp.where(jnp.arange(BLOCKS) == fuller, CAP, jnp.minimum(one_draw, two_draw)).astype(jnp.int32)


def draw_neighbours(key, part):
    width_all = 3 * BLK_DEV
    own_block = (jnp.arange(BLOCKS) % BLK_DEV)[:, None]
    candidate = jnp.arange(width_all)[None, :]
    nearby = jnp.abs(candidate % BLK_DEV - own_block) <= 1
    itself = (candidate // BLK_DEV == 1) & (candidate % BLK_DEV == own_block)
    scores = jax.random.randint(jax.random.fold_in(key, 23), (BLOCKS, width_all), 0, 65536) * 64 + candidate
    scores = jnp.where(nearby, scores, -1)
    scores = jnp.where(itself, 1 << 24, scores)
    ranked, chosen = lax.top_k(scores, NB)
    return chosen.astype(jnp.int32)


def draw_wavevectors(key, part):
    values = jax.random.randint(jax.random.fold_in(key, 37), (3, K), -4, 5)
    vacant = jnp.all(values == 0, axis=0)
    first_row = jnp.where(vacant, 1, values[0])
    return jnp.concatenate([first_row[None], values[1:]], 0).astype(jnp.int32)


def levels(own_key, shape, pieces, least, top_value):
    loudness, own = 1.0, jax.random.fold_in(own_key, 6)
    for axis_at, blocks in pieces:
        draws = jnp.exp(jax.random.uniform(jax.random.fold_in(own, axis_at), (blocks,), jnp.float32, least / len(pieces), top_value / len(pieces)))
        loudness = loudness * jnp.repeat(draws, shape[axis_at] // blocks).reshape([-1 if axis == axis_at else 1 for axis in range(len(shape))])
    return loudness


def gaussian(own_key, extent, spread, most, shards=(), kind=jnp.bfloat16):
    values = spread * jax.random.normal(own_key, extent, jnp.float32)
    if shards:
        values = values * levels(own_key, extent, shards, -0.22, 0.18)
    return jnp.clip(values, -most, most).astype(kind)


def setup_inputs(seed: int = 0) -> dict:
    arg_keys = jax.random.split(jax.random.key(seed), 8)
    return {
        "features": gaussian(arg_keys[0], (C, SLOTS), 1.0, 6.0, ((0, 4), (1, 8)), jnp.float32),
        "positions": draw_positions(jax.random.fold_in(arg_keys[7], 71), 0),
        "counts": draw_counts(jax.random.fold_in(arg_keys[7], 71), 0),
        "neighbours": draw_neighbours(jax.random.fold_in(arg_keys[7], 71), 0),
        "wavevectors": draw_wavevectors(jax.random.fold_in(arg_keys[7], 71), 0),
        "filters": gaussian(arg_keys[5], (NRAD, C, C), (NRAD * C) ** -0.5, 0.125, ((1, 4),), jnp.float32),
        "cotangent": gaussian(arg_keys[6], (C, SLOTS), 1.0, 6.0, ((0, 4), (1, 8)), jnp.float32),
    }


slab_width = 1.0
pair_scale = 0.3
screen_alpha = 2000.0
screen_kappa = 100.0
wave_most = 128
highest = lax.Precision.HIGHEST

def radial_terms(own_place, far_place, offset):
    delta_x = own_place[0][:, None] - (far_place[0][None, :] + offset * slab_width)
    delta_y = own_place[1][:, None] - far_place[1][None, :]
    delta_z = own_place[2][:, None] - far_place[2][None, :]
    square = delta_x * delta_x + delta_y * delta_y + delta_z * delta_z
    distance = jnp.sqrt(square)
    envelope = jnp.maximum(1.0 - square, 0.0) ** 2
    centres = jnp.arange(NRAD, dtype=jnp.float32) + 0.5
    scaled = distance[None] * NRAD - centres[:, None, None]
    return pair_scale * jnp.exp(-0.5 * scaled * scaled) * envelope[None]

def wave_table(wavevectors, x_length, y_length):
    lengths = jnp.array([x_length, y_length, 1.0], jnp.float32)
    scaled = 2.0 * math.pi * wavevectors.astype(jnp.float32) / lengths[:, None]
    square = lax.optimization_barrier(jnp.sum(scaled * scaled, 0))
    screened = jnp.exp(-square / screen_alpha) / (square + screen_kappa)
    return (scaled, screened / jnp.sqrt(jnp.sum(screened * screened)))

def phase_block(wave_part, coords):
    return wave_part[0][:, None] * coords[0][None, :] + wave_part[1][:, None] * coords[1][None, :] + wave_part[2][:, None] * coords[2][None, :]

def structure(fields, coords, scaled):
    wave_block = min(K, wave_most)
    real_list = []
    imag_list = []
    for first_wave in range(0, K, wave_block):
        phases = phase_block(scaled[:, first_wave:first_wave + wave_block], coords)
        real_list.append(jnp.einsum('ci,ki->ck', fields, jnp.cos(phases), precision=highest))
        imag_list.append(jnp.einsum('ci,ki->ck', fields, jnp.sin(phases), precision=highest))
    return (jnp.concatenate(real_list, 1), jnp.concatenate(imag_list, 1))

def project_back(real_part, imag_part, coords, scaled, weights, factor):
    wave_block = min(K, wave_most)
    result = jnp.zeros((real_part.shape[0], coords.shape[1]), jnp.float32)
    for first_wave in range(0, K, wave_block):
        phases = phase_block(scaled[:, first_wave:first_wave + wave_block], coords)
        chosen = weights[first_wave:first_wave + wave_block]
        result = result + jnp.einsum('ck,ki->ci', real_part[:, first_wave:first_wave + wave_block] * chosen[None], jnp.cos(phases), precision=highest)
        result = result + jnp.einsum('ck,ki->ci', imag_part[:, first_wave:first_wave + wave_block] * chosen[None], jnp.sin(phases), precision=highest)
    return factor * result

def reference(features, positions, counts, neighbours, wavevectors, filters, cotangent):
    slots_layer = BLK_DEV * CAP
    slot_index = jnp.arange(SLOTS, dtype=jnp.int32)
    live_mask = (slot_index % CAP < jnp.repeat(counts, CAP, total_repeat_length=SLOTS)).astype(jnp.float32)
    masked = features * live_mask[None]
    cot_masked = cotangent * live_mask[None]

    def source_of(block_number, chosen):
        own_layer = block_number // BLK_DEV
        section = chosen // BLK_DEV
        source_layer = (own_layer + section - 1 + N_SPACE) % N_SPACE
        first_slot = ((source_layer * BLK_DEV + chosen % BLK_DEV) * CAP).astype(jnp.int32)
        return (first_slot, (section - 1).astype(jnp.float32))

    def pair_forward(block_number):
        own_place = lax.dynamic_slice_in_dim(positions, (block_number * CAP).astype(jnp.int32), CAP, 1)
        running = jnp.zeros((NRAD, C, CAP), jnp.float32)
        for entry_index in range(NB):
            first_slot, offset = source_of(block_number, neighbours[block_number, entry_index])
            far_place = lax.dynamic_slice_in_dim(positions, first_slot, CAP, 1)
            values = lax.dynamic_slice_in_dim(masked, first_slot, CAP, 1)
            radial = radial_terms(own_place, far_place, offset)
            running = running + jnp.einsum('cj,rij->rci', values, radial, precision=highest)
        return jnp.einsum('rcd,rci->di', filters, running, precision=highest)
    pre_blocks = lax.map(pair_forward, jnp.arange(BLOCKS, dtype=jnp.int32))
    pre = jnp.transpose(pre_blocks, (1, 0, 2)).reshape(C, SLOTS)
    layer_of = (slot_index // slots_layer).astype(jnp.float32)
    coords = jnp.stack([positions[0] + layer_of * slab_width, positions[1], positions[2]])
    scaled, weights = wave_table(wavevectors, N_SPACE * slab_width, BLK_DEV * 1.0)
    factor = math.sqrt(3.0 / SLOTS)
    real_part, imag_part = structure(masked, coords, scaled)
    long_forward = project_back(real_part, imag_part, coords, scaled, weights, factor)
    sigma = jax.nn.sigmoid(pre)
    updated = live_mask[None] * (masked + pre * sigma + long_forward)
    upstream = cot_masked * sigma * (1.0 + pre * (1.0 - sigma))

    def pair_backward(gradient, block_number):
        own_place = lax.dynamic_slice_in_dim(positions, (block_number * CAP).astype(jnp.int32), CAP, 1)
        cot_block = lax.dynamic_slice_in_dim(upstream, (block_number * CAP).astype(jnp.int32), CAP, 1)
        pair_cot = jnp.einsum('rcd,di->rci', filters, cot_block, precision=highest)
        for entry_index in range(NB):
            first_slot, offset = source_of(block_number, neighbours[block_number, entry_index])
            far_place = lax.dynamic_slice_in_dim(positions, first_slot, CAP, 1)
            radial = radial_terms(own_place, far_place, offset)
            contribution = jnp.einsum('rci,rij->cj', pair_cot, radial, precision=highest)
            current = lax.dynamic_slice_in_dim(gradient, first_slot, CAP, 1)
            gradient = lax.dynamic_update_slice_in_dim(gradient, current + contribution, first_slot, 1)
        return (gradient, None)
    pair_grad, _ = lax.scan(pair_backward, jnp.zeros((C, SLOTS), jnp.float32), jnp.arange(BLOCKS, dtype=jnp.int32))
    real_cot, imag_cot = structure(cot_masked, coords, scaled)
    long_adjoint = project_back(real_cot, imag_cot, coords, scaled, weights, factor)
    grad_features = live_mask[None] * (cot_masked + pair_grad + long_adjoint)
    return (updated, grad_features)
```

```python
import functools
import math

import jax
import jax.numpy as jnp
from jax import lax
from jax.experimental import pallas as pl
from jax.experimental.pallas import tpu as pltpu
from jax.sharding import PartitionSpec as P

NRAD = 8
NB = 4
BLK_DEV = 2
MOST = 4
SIDE = 2 * MOST + 1
HALF = (SIDE**3 - 1) // 2
MESH = pl.DeviceIdType.MESH
f32 = jnp.float32
bf16 = jnp.bfloat16


def halves(x):
    high = x.astype(bf16)
    return high, (x - high.astype(f32)).astype(bf16)


def dot(a, b):
    return jnp.dot(a, b, preferred_element_type=f32)


def dot_nt(a, b):
    return lax.dot_general(a, b, (((1,), (1,)), ((), ())), preferred_element_type=f32)


def turn_cos_sin(p):
    r = (p - jnp.floor(p + 0.5)) * math.pi
    s2 = r * r
    s = 1.0 / 6227020800.0
    for n in (-1.0 / 39916800.0, 1.0 / 362880.0, -1.0 / 5040.0, 1.0 / 120.0, -1.0 / 6.0, 1.0):
        s = s * s2 + n
    s = s * r
    c = 1.0 / 479001600.0
    for n in (-1.0 / 3628800.0, 1.0 / 40320.0, -1.0 / 720.0, 1.0 / 24.0, -0.5, 1.0):
        c = c * s2 + n
    return 1.0 - 2.0 * s * s, 2.0 * s * c


def lattice(first, rows):
    f = lax.broadcasted_iota(jnp.int32, (rows, 1), 0).astype(f32) + (first + HALF + 1.0)
    a = jnp.floor((f + 0.5) * (1.0 / (SIDE * SIDE)))
    rest = f - a * (SIDE * SIDE)
    b = jnp.floor((rest + 0.5) * (1.0 / SIDE))
    c = rest - b * SIDE
    return f, a - MOST, b - MOST, c - MOST


def kernel(n, chans, feat, pos, counts, nbr, wv, filt, cot, upd, grad,
           f6, p6, pt, fx, cm, c2, gh, gl, mt, mts, th, tl, ss, rb, sg, ps, rx, ug, so, sr,
           re, wo, wp, rw, rt, hb, misc_s, misc_r, red_s, red_r, gat_s, gat_r):
    panel, slots = feat.shape
    cap = slots // BLK_DEV
    rows_all = th.shape[0]
    lat = rows_all // 2
    piece = ss.shape[1]
    pair = 2 * panel
    groups = chans // 2
    s = lax.axis_index("space")
    q = lax.axis_index("chan")
    p = lax.rem(q, 2)
    h = lax.div(q, 2)
    mate = (s, q + 1 - 2 * p)
    nxt = (lax.rem(s + 1, n), q)
    prv = (lax.rem(s + n - 1, n), q)

    def remote(src, dst, at, dev):
        return pltpu.make_async_remote_copy(
            src_ref=src, dst_ref=dst, send_sem=misc_s.at[at], recv_sem=misc_r.at[at],
            device_id=dev, device_id_type=MESH)

    lane = lax.broadcasted_iota(jnp.int32, (1, slots), 1)
    bound = jnp.where(lane < cap, counts[0], counts[1] + cap)
    live = (lane < bound).astype(f32)
    fm = feat[...] * live
    cmask = cot[...] * live
    f6[1, 0] = fm
    for b in range(BLK_DEV):
        cm[b] = cmask[:, b * cap:(b + 1) * cap]
    p6[1] = jnp.zeros(p6.shape[1:], f32)
    for b in range(BLK_DEV):
        p6[1, b, 0:3, :] = pos[:, b * cap:(b + 1) * cap]

    barrier = pltpu.get_barrier_semaphore()

    def greet(k, carry):
        pl.semaphore_signal(barrier, inc=1, device_id=(lax.rem(s + k, n), q), device_id_type=MESH)
        return carry

    lax.fori_loop(1, n, greet, 0)
    pl.semaphore_signal(barrier, inc=1, device_id=mate, device_id_type=MESH)
    for k in range(1, groups):
        pl.semaphore_signal(barrier, inc=1, device_id=(s, lax.rem(q + 2 * k, chans)), device_id_type=MESH)
    pl.semaphore_wait(barrier, n - 1 + 1 + groups - 1)

    pos_up = remote(p6.at[1], p6.at[0], 0, nxt)
    pos_dn = remote(p6.at[1], p6.at[2], 1, prv)
    feat_up = remote(f6.at[1, 0], f6.at[0, 0], 2, nxt)
    feat_dn = remote(f6.at[1, 0], f6.at[2, 0], 3, prv)
    feat_mate = remote(f6.at[1, 0], f6.at[1, 1], 4, mate)
    fwd_lo = remote(f6.at[0, 0], f6.at[0, 1], 5, mate)
    fwd_hi = remote(f6.at[2, 0], f6.at[2, 1], 6, mate)
    filt_mate = remote(filt, fx, 7, mate)
    cot_mate = remote(cm.at[1 - p], c2.at[p], 8, mate)
    for c in (pos_up, pos_dn, feat_up, feat_dn, feat_mate, filt_mate, cot_mate):
        c.start()
    c2[p] = cm[p]

    chunk = 16
    layer_x = s.astype(f32)
    xs = (pos[0:1, :] + layer_x) * (1.0 / n)
    ys = pos[1:2, :] * (1.0 / BLK_DEV)
    zs = pos[2:3, :]

    def table(i, carry):
        at = pl.multiple_of(i * chunk, chunk)
        _, a, b, c = lattice((i * chunk).astype(f32), chunk)
        cosv, sinv = turn_cos_sin(a * xs + b * ys + c * zs)
        ch, cl = halves(cosv)
        sh, sl = halves(sinv)
        th[pl.ds(at, chunk), :] = ch
        tl[pl.ds(at, chunk), :] = cl
        th[pl.ds(lat + at, chunk), :] = sh
        tl[pl.ds(lat + at, chunk), :] = sl
        return carry

    lax.fori_loop(0, lat // chunk, table, 0)
    vh, vl = halves(jnp.concatenate([fm, cmask], 0))
    two = dot_nt(th[...], jnp.concatenate([vh, vl], 0))
    full = two[:, :pair] + two[:, pair:] + dot_nt(tl[...], vh)
    ss[...] = full.reshape(n, piece, pair)

    def reduce_copy(k):
        return pltpu.make_async_remote_copy(
            src_ref=ss.at[lax.rem(s + k, n)], dst_ref=rb.at[s], send_sem=red_s.at[k],
            recv_sem=red_r.at[k], device_id=(lax.rem(s + k, n), q), device_id_type=MESH)

    def start_reduce(k, carry):
        reduce_copy(k).start()
        return carry

    feat_up.wait_recv()
    fwd_lo.start()
    feat_dn.wait_recv()
    fwd_hi.start()
    lax.fori_loop(1, n, start_reduce, 0)

    pos_up.wait_recv()
    pos_dn.wait_recv()
    pt[...] = p6[1, p].T
    step = 16
    chosen = [nbr[p, e] for e in range(NB)]

    def radial(i, carry):
        at = pl.multiple_of(i * step, step)
        own = pt[pl.ds(at, step), :]
        for e in range(NB):
            w = chosen[e]
            far = p6[lax.div(w, BLK_DEV), lax.rem(w, BLK_DEV)]
            offset = (lax.div(w, BLK_DEV) - 1).astype(f32)
            dx = own[:, 0:1] - (far[0:1, :] + offset)
            dy = own[:, 1:2] - far[1:2, :]
            dz = own[:, 2:3] - far[2:3, :]
            sq = jnp.minimum(dx * dx + dy * dy + dz * dz, 1.0)
            left = 1.0 - sq
            u = NRAD * jnp.sqrt(sq) - 0.5
            t = jnp.exp(u)
            g = jnp.exp(-0.5 * u * u) * (0.3 * left * left)
            for r in range(NRAD):
                if r:
                    g = g * (t * math.exp(0.5 - r))
                a, b = halves(g)
                gh[r, pl.ds(at, step), e * cap:(e + 1) * cap] = a
                gl[r, pl.ds(at, step), e * cap:(e + 1) * cap] = b
        return carry

    lax.fori_loop(0, cap // step, radial, 0)

    feat_mate.wait_recv()
    fwd_lo.wait_recv()
    fwd_hi.wait_recv()
    for layer in range(3):
        both = jnp.concatenate([f6[layer, 0], f6[layer, 1]], 0)
        for b in range(BLK_DEV):
            a, c = halves(both[:, b * cap:(b + 1) * cap].T)
            mt[layer * BLK_DEV + b] = jnp.concatenate([a, c], 1)
    for e in range(NB):
        mts[e * cap:(e + 1) * cap, :] = mt[chosen[e]]
    filt_mate.wait_recv()

    def filters_of(r):
        return halves(jnp.concatenate([filt[r], fx[r]], 0))

    def forward(r, total):
        two = dot(gh[r], mts[...])
        sums = two[:, :pair] + two[:, pair:] + dot(gl[r], mts[:, :pair])
        a, b = halves(sums)
        fh, fl = filters_of(r)
        return total + dot(jnp.concatenate([a, b], 1), jnp.concatenate([fh, fh], 0)) + dot(a, fl)

    total = lax.fori_loop(0, NRAD, forward, jnp.zeros((cap, groups * pair), f32))
    for k in range(groups):
        ps[k] = total[:, k * pair:(k + 1) * pair]
    pre_copies = []
    for k in range(1, groups):
        c = remote(ps.at[lax.rem(h + k, groups)], rx.at[k - 1], 16 + k, (s, lax.rem(q + 2 * k, chans)))
        c.start()
        pre_copies.append(c)

    def wait_reduce(k, carry):
        reduce_copy(k).wait_recv()
        return carry

    lax.fori_loop(1, n, wait_reduce, 0)
    rb[s] = ss[s]

    def add_up(k, acc):
        return acc + rb[k]

    sg[s] = lax.fori_loop(0, n, add_up, jnp.zeros((piece, pair), f32))

    def gather_copy(k):
        return pltpu.make_async_remote_copy(
            src_ref=sg.at[s], dst_ref=sg.at[s], send_sem=gat_s.at[k],
            recv_sem=gat_r.at[k], device_id=(lax.rem(s + k, n), q), device_id_type=MESH)

    def start_gather(k, carry):
        gather_copy(k).start()
        return carry

    lax.fori_loop(1, n, start_gather, 0)

    for c in pre_copies:
        c.wait_recv()
    acc = ps[h]
    for k in range(1, groups):
        acc = acc + rx[k - 1]
    pre = acc.T
    cot_mate.wait_recv()
    sigma = 1.0 / (1.0 + jnp.exp(-pre))
    act = pre * sigma
    ug[h] = jnp.concatenate([c2[0], c2[1]], 0) * sigma * (1.0 + pre * (1.0 - sigma))
    up_copies = []
    for k in range(1, groups):
        c = pltpu.make_async_remote_copy(
            src_ref=ug.at[h], dst_ref=ug.at[h], send_sem=misc_s.at[24 + k], recv_sem=misc_r.at[24 + k],
            device_id=(s, lax.rem(q + 2 * k, chans)), device_id_type=MESH)
        c.start()
        up_copies.append(c)
    so[0] = act[:panel]
    so[1] = act[panel:]
    act_mate = remote(so.at[1 - p], sr, 9, mate)
    act_mate.start()

    f, a, b, c = lattice(0.0, lat)
    wf = wv[...].astype(f32) + MOST
    key = (wf[0:1] * SIDE + wf[1:2]) * SIDE + wf[2:3]
    hit = (key == f).astype(f32) + ((2.0 * HALF - key) == f).astype(f32)
    times = jnp.sum(hit, axis=1, keepdims=True)
    qa = a * (2.0 * math.pi / n)
    qb = b * (2.0 * math.pi / BLK_DEV)
    qc = c * (2.0 * math.pi)
    k2 = qa * qa + qb * qb + qc * qc
    raw = jnp.exp(-k2 / 2000.0) / (k2 + 100.0)
    norm = jnp.sum(times * raw * raw, axis=0, keepdims=True)
    weight = times * raw * lax.rsqrt(norm) * math.sqrt(3.0 / (n * slots))
    weight = jnp.concatenate([weight, weight], 0)

    def wait_gather(k, carry):
        gather_copy(k).wait_recv()
        return carry

    lax.fori_loop(1, n, wait_gather, 0)
    sh, sl = halves((sg[...].reshape(rows_all, pair) * weight).T)
    two = dot(jnp.concatenate([sh, sl], 0), th[...])
    far_part = two[:pair] + two[pair:] + dot(sh, tl[...])

    for c in up_copies:
        c.wait_recv()
    uh, ul = halves(ug[...].reshape(groups * pair, cap))
    re[...] = jnp.zeros(re.shape, f32)

    def backward(r, carry):
        fh, fl = filters_of(r)
        two = dot(jnp.concatenate([fh, fl], 0), uh)
        a, b = halves(two[:pair] + two[pair:] + dot(fh, ul))
        out = dot(jnp.concatenate([a, b], 0), gh[r])
        re[...] += out[:pair] + out[pair:] + dot(a, gl[r])
        return carry

    lax.fori_loop(0, NRAD, backward, 0)
    for w in range(3 * BLK_DEV):
        acc = jnp.zeros((pair, cap), f32)
        for e in range(NB):
            acc = acc + jnp.where(chosen[e] == w, re[:, e * cap:(e + 1) * cap], 0.0)
        wo[w] = acc[:panel]
        wp[w] = acc[panel:]
    ret_mate = remote(wp, rw, 10, mate)
    ret_mate.start()

    act_mate.wait_recv()
    mine, other = so[p], sr[...]
    first = jnp.where(p == 0, mine, other)
    second = jnp.where(p == 0, other, mine)
    upd[...] = live * (fm + jnp.concatenate([first, second], 1) + far_part[:panel])

    ret_mate.wait_recv()
    for w in range(3 * BLK_DEV):
        rt[w // BLK_DEV, w % BLK_DEV] = wo[w] + rw[w]
    ret_up = remote(rt.at[2], hb.at[0], 11, nxt)
    ret_dn = remote(rt.at[0], hb.at[1], 12, prv)
    ret_up.start()
    ret_dn.start()
    part = cmask + far_part[panel:]
    ret_up.wait_recv()
    ret_dn.wait_recv()
    near = [rt[1, b] + hb[0, b] + hb[1, b] for b in range(BLK_DEV)]
    grad[...] = live * (part + jnp.concatenate(near, 1))

    for c in (pos_up, pos_dn, feat_up, feat_dn, feat_mate, fwd_lo, fwd_hi, filt_mate, cot_mate,
              act_mate, ret_mate, ret_up, ret_dn, *pre_copies, *up_copies):
        c.wait_send()

    def drain(k, carry):
        reduce_copy(k).wait_send()
        gather_copy(k).wait_send()
        return carry

    lax.fori_loop(1, n, drain, 0)


def shards(n, chans, features, positions, counts, neighbours, wavevectors, filters, cotangent):
    panel, slots = features.shape
    cap = slots // BLK_DEV
    pair = 2 * panel
    groups = chans // 2
    piece = -(-(-(-2 * HALF // n)) // 8) * 8
    while (n * piece) % 32:
        piece += 8
    rows = n * piece
    vm = pltpu.VMEM
    scratch = [
        vm((3, 2, panel, slots), f32),
        vm((3, BLK_DEV, 8, cap), f32),
        vm((cap, 8), f32),
        vm(filters.shape, f32),
        vm((BLK_DEV, panel, cap), f32),
        vm((2, panel, cap), f32),
        vm((NRAD, cap, NB * cap), bf16),
        vm((NRAD, cap, NB * cap), bf16),
        vm((3 * BLK_DEV, cap, 2 * pair), bf16),
        vm((NB * cap, 2 * pair), bf16),
        vm((rows, slots), bf16),
        vm((rows, slots), bf16),
        vm((n, piece, pair), f32),
        vm((n, piece, pair), f32),
        vm((n, piece, pair), f32),
        vm((groups, cap, pair), f32),
        vm((max(groups - 1, 1), cap, pair), f32),
        vm((groups, pair, cap), f32),
        vm((2, panel, cap), f32),
        vm((panel, cap), f32),
        vm((pair, NB * cap), f32),
        vm((3 * BLK_DEV, panel, cap), f32),
        vm((3 * BLK_DEV, panel, cap), f32),
        vm((3 * BLK_DEV, panel, cap), f32),
        vm((3, BLK_DEV, panel, cap), f32),
        vm((2, BLK_DEV, panel, cap), f32),
        pltpu.SemaphoreType.DMA((32,)),
        pltpu.SemaphoreType.DMA((32,)),
        pltpu.SemaphoreType.DMA((n,)),
        pltpu.SemaphoreType.DMA((n,)),
        pltpu.SemaphoreType.DMA((n,)),
        pltpu.SemaphoreType.DMA((n,)),
    ]
    whole = pl.BlockSpec(memory_space=pltpu.VMEM)
    small = pl.BlockSpec(memory_space=pltpu.SMEM)
    out = jax.ShapeDtypeStruct((panel, slots), f32)
    return pl.pallas_call(
        functools.partial(kernel, n, chans),
        out_shape=(out, out),
        in_specs=[whole, whole, small, small, whole, whole, whole],
        out_specs=(whole, whole),
        scratch_shapes=scratch,
        compiler_params=pltpu.CompilerParams(
            collective_id=0, has_side_effects=True, vmem_limit_bytes=48 * 1024 * 1024),
    )(features, positions, counts, neighbours, wavevectors, filters, cotangent)


def solution(mesh):
    return jax.shard_map(
        functools.partial(shards, mesh.shape["space"], mesh.shape["chan"]),
        mesh=mesh,
        in_specs=(
            P("chan", "space"),
            P(None, "space"),
            P("space"),
            P("space", None),
            P(),
            P(None, "chan", None),
            P("chan", "space"),
        ),
        out_specs=(P("chan", "space"), P("chan", "space")),
        check_vma=False,
    )
```

```python
import functools
import math

import jax
import jax.numpy as jnp
from jax import lax
from jax.experimental import pallas as pl
from jax.experimental.pallas import tpu as pltpu
from jax.sharding import PartitionSpec as P

NRAD = 8
NB = 4
BLK_DEV = 2
PARTS = 2
MOST = 4
SIDE = 2 * MOST + 1
HALF = (SIDE**3 - 1) // 2
MESH = pl.DeviceIdType.MESH
f32 = jnp.float32
bf16 = jnp.bfloat16


def halves(x):
    high = x.astype(bf16)
    return high, (x - high.astype(f32)).astype(bf16)


def dot(a, b):
    return jnp.dot(a, b, preferred_element_type=f32)


def dot_nt(a, b):
    return lax.dot_general(a, b, (((1,), (1,)), ((), ())), preferred_element_type=f32)


def turn_cos_sin(p):
    r = (p - jnp.floor(p + 0.5)) * math.pi
    s2 = r * r
    s = 1.0 / 6227020800.0
    for n in (-1.0 / 39916800.0, 1.0 / 362880.0, -1.0 / 5040.0, 1.0 / 120.0, -1.0 / 6.0, 1.0):
        s = s * s2 + n
    s = s * r
    c = 1.0 / 479001600.0
    for n in (-1.0 / 3628800.0, 1.0 / 40320.0, -1.0 / 720.0, 1.0 / 24.0, -0.5, 1.0):
        c = c * s2 + n
    return 1.0 - 2.0 * s * s, 2.0 * s * c


def lattice(first, rows):
    f = lax.broadcasted_iota(jnp.int32, (rows, 1), 0).astype(f32) + (first + HALF + 1.0)
    a = jnp.floor((f + 0.5) * (1.0 / (SIDE * SIDE)))
    rest = f - a * (SIDE * SIDE)
    b = jnp.floor((rest + 0.5) * (1.0 / SIDE))
    c = rest - b * SIDE
    return f, a - MOST, b - MOST, c - MOST


def kernel(n, chans, feat_in, pos_in, counts_in, nbr_in, wv_in, filt_in, cot_in, upd, grad,
           feat, pos, counts, nbr, wv, filt, cot,
           f6, p6, pt, fx, fh, fl, cm, c2, gh, gl, mts, mt, th, tl, ss, rb, sg, ps, rx, ug, so, sr,
           re, wo, wp, rw, rt, hb, load_s, misc_s, misc_r, red_s, red_r, gat_s, gat_r):
    loads = [
        pltpu.make_async_copy(a, b, load_s.at[i])
        for i, (a, b) in enumerate(zip(
            (feat_in, pos_in, counts_in, nbr_in, wv_in, filt_in, cot_in),
            (feat, pos, counts, nbr, wv, filt, cot)))
    ]
    for c in loads:
        c.start()
    panel, slots = feat.shape
    cap = slots // BLK_DEV
    rows_all = th.shape[0]
    lat = rows_all // 2
    piece = ss.shape[1]
    pair = 2 * panel
    groups = chans // 2
    s = lax.axis_index("space")
    q = lax.axis_index("chan")
    p = lax.rem(q, 2)
    h = lax.div(q, 2)
    mate = (s, q + 1 - 2 * p)
    nxt = (lax.rem(s + 1, n), q)
    prv = (lax.rem(s + n - 1, n), q)

    def remote(src, dst, at, dev):
        return pltpu.make_async_remote_copy(
            src_ref=src, dst_ref=dst, send_sem=misc_s.at[at], recv_sem=misc_r.at[at],
            device_id=dev, device_id_type=MESH)

    barrier = pltpu.get_barrier_semaphore()

    def greet(k, carry):
        pl.semaphore_signal(barrier, inc=1, device_id=(lax.rem(s + k, n), q), device_id_type=MESH)
        return carry

    lax.fori_loop(1, n, greet, 0)
    pl.semaphore_signal(barrier, inc=1, device_id=mate, device_id_type=MESH)
    for k in range(1, groups):
        pl.semaphore_signal(barrier, inc=1, device_id=(s, lax.rem(q + 2 * k, chans)), device_id_type=MESH)

    for at in (0, 1, 2, 6):
        loads[at].wait()
    lane = lax.broadcasted_iota(jnp.int32, (1, slots), 1)
    bound = jnp.where(lane < cap, counts[0], counts[1] + cap)
    live = (lane < bound).astype(f32)
    fm = feat[...] * live
    cmask = cot[...] * live
    f6[1, 0] = fm
    for b in range(BLK_DEV):
        cm[b] = cmask[:, b * cap:(b + 1) * cap]
    p6[1] = jnp.zeros(p6.shape[1:], f32)
    for b in range(BLK_DEV):
        p6[1, b, 0:3, :] = pos[:, b * cap:(b + 1) * cap]

    pl.semaphore_wait(barrier, n - 1 + 1 + groups - 1)

    pos_up = remote(p6.at[1], p6.at[0], 0, nxt)
    pos_dn = remote(p6.at[1], p6.at[2], 1, prv)
    feat_up = remote(f6.at[1, 0], f6.at[0, 0], 2, nxt)
    feat_dn = remote(f6.at[1, 0], f6.at[2, 0], 3, prv)
    feat_mate = remote(f6.at[1, 0], f6.at[1, 1], 4, mate)
    fwd_lo = remote(f6.at[0, 0], f6.at[0, 1], 5, mate)
    fwd_hi = remote(f6.at[2, 0], f6.at[2, 1], 6, mate)
    filt_mate = remote(filt_in, fx, 7, mate)
    cot_mate = remote(cm.at[1 - p], c2.at[p], 8, mate)
    for c in (pos_up, pos_dn, feat_up, feat_dn, feat_mate, filt_mate, cot_mate):
        c.start()
    c2[p] = cm[p]

    chunk = 16
    layer_x = s.astype(f32)
    xs = (pos[0:1, :] + layer_x) * (1.0 / n)
    ys = pos[1:2, :] * (1.0 / BLK_DEV)
    zs = pos[2:3, :]

    def table(i, carry):
        at = pl.multiple_of(i * chunk, chunk)
        _, a, b, c = lattice((i * chunk).astype(f32), chunk)
        cosv, sinv = turn_cos_sin(a * xs + b * ys + c * zs)
        ch, cl = halves(cosv)
        sh, sl = halves(sinv)
        th[pl.ds(at, chunk), :] = ch
        tl[pl.ds(at, chunk), :] = cl
        th[pl.ds(lat + at, chunk), :] = sh
        tl[pl.ds(lat + at, chunk), :] = sl
        return carry

    lax.fori_loop(0, lat // chunk, table, 0)
    vh, vl = halves(jnp.concatenate([fm, cmask], 0))
    two = dot_nt(th[...], jnp.concatenate([vh, vl], 0))
    full = two[:, :pair] + two[:, pair:] + dot_nt(tl[...], vh)
    ss[...] = full.reshape(n, piece, pair)

    def reduce_copy(k):
        return pltpu.make_async_remote_copy(
            src_ref=ss.at[lax.rem(s + k, n)], dst_ref=rb.at[s], send_sem=red_s.at[k],
            recv_sem=red_r.at[k], device_id=(lax.rem(s + k, n), q), device_id_type=MESH)

    def start_reduce(k, carry):
        reduce_copy(k).start()
        return carry

    feat_up.wait_recv()
    fwd_lo.start()
    feat_dn.wait_recv()
    fwd_hi.start()
    lax.fori_loop(1, n, start_reduce, 0)

    pos_up.wait_recv()
    pos_dn.wait_recv()
    pt[...] = p6[1, p].T
    loads[3].wait()
    step = 16
    part_i = cap // PARTS
    chosen = [nbr[p, e] for e in range(NB)]

    for half in range(PARTS):
        def radial(i, carry):
            at = pl.multiple_of(i * step, step)
            own = pt[pl.ds(half * part_i + at, step), :]
            for e in range(NB):
                w = chosen[e]
                far = p6[lax.div(w, BLK_DEV), lax.rem(w, BLK_DEV)]
                offset = (lax.div(w, BLK_DEV) - 1).astype(f32)
                dx = own[:, 0:1] - (far[0:1, :] + offset)
                dy = own[:, 1:2] - far[1:2, :]
                dz = own[:, 2:3] - far[2:3, :]
                sq = jnp.minimum(dx * dx + dy * dy + dz * dz, 1.0)
                left = 1.0 - sq
                u = NRAD * jnp.sqrt(sq) - 0.5
                t = jnp.exp(u)
                g = jnp.exp(-0.5 * u * u) * (0.3 * left * left)
                for r in range(NRAD):
                    if r:
                        g = g * (t * math.exp(0.5 - r))
                    a, b = halves(g)
                    gh[half, pl.ds(r * part_i + at, step), e * cap:(e + 1) * cap] = a
                    gl[half, pl.ds(r * part_i + at, step), e * cap:(e + 1) * cap] = b
            return carry

        lax.fori_loop(0, part_i // step, radial, 0)

    feat_mate.wait_recv()
    fwd_lo.wait_recv()
    fwd_hi.wait_recv()
    for layer in range(3):
        both = jnp.concatenate([f6[layer, 0], f6[layer, 1]], 0)
        for b in range(BLK_DEV):
            a, c = halves(both[:, b * cap:(b + 1) * cap].T)
            mt[layer * BLK_DEV + b] = jnp.concatenate([a, c], 1)
    for e in range(NB):
        mts[e * cap:(e + 1) * cap, :] = mt[chosen[e]]
    filt_mate.wait_recv()
    loads[5].wait()
    for r in range(NRAD):
        for i, src in enumerate((filt, fx)):
            a, b = halves(src[r])
            at = r * pair + i * panel
            fh[at:at + panel, :] = a
            fl[at:at + panel, :] = b

    pre_copies = []
    for half in range(PARTS):
        two = dot(gh[half], mts[...])
        sums = two[:, :pair] + two[:, pair:] + dot(gl[half], mts[:, :pair])
        a, b = halves(sums)
        total = None
        for r in range(NRAD):
            here = slice(r * part_i, (r + 1) * part_i)
            wh, wl = fh[r * pair:(r + 1) * pair, :], fl[r * pair:(r + 1) * pair, :]
            term = dot(jnp.concatenate([a[here], b[here]], 1), jnp.concatenate([wh, wh], 0)) + dot(a[here], wl)
            total = term if r == 0 else total + term
        for k in range(groups):
            ps[half, k] = total[:, k * pair:(k + 1) * pair]
        copies = []
        for k in range(1, groups):
            c = remote(ps.at[half, lax.rem(h + k, groups)], rx.at[half, k - 1], 16 + half * groups + k,
                       (s, lax.rem(q + 2 * k, chans)))
            c.start()
            copies.append(c)
        pre_copies.append(copies)

    def wait_reduce(k, carry):
        reduce_copy(k).wait_recv()
        return carry

    lax.fori_loop(1, n, wait_reduce, 0)
    rb[s] = ss[s]

    def add_up(k, acc):
        return acc + rb[k]

    sg[s] = lax.fori_loop(0, n, add_up, jnp.zeros((piece, pair), f32))

    def gather_copy(k):
        return pltpu.make_async_remote_copy(
            src_ref=sg.at[s], dst_ref=sg.at[s], send_sem=gat_s.at[k],
            recv_sem=gat_r.at[k], device_id=(lax.rem(s + k, n), q), device_id_type=MESH)

    def start_gather(k, carry):
        gather_copy(k).start()
        return carry

    lax.fori_loop(1, n, start_gather, 0)

    cot_mate.wait_recv()
    up_copies = []
    for half in range(PARTS):
        here = slice(half * part_i, (half + 1) * part_i)
        for c in pre_copies[half]:
            c.wait_recv()
        acc = ps[half, h]
        for k in range(1, groups):
            acc = acc + rx[half, k - 1]
        pre = acc.T
        sigma = 1.0 / (1.0 + jnp.exp(-pre))
        act = pre * sigma
        ug[half, h] = jnp.concatenate([c2[0, :, here], c2[1, :, here]], 0) * sigma * (1.0 + pre * (1.0 - sigma))
        copies = []
        for k in range(1, groups):
            c = pltpu.make_async_remote_copy(
                src_ref=ug.at[half, h], dst_ref=ug.at[half, h], send_sem=misc_s.at[16 + (PARTS + half) * groups + k],
                recv_sem=misc_r.at[16 + (PARTS + half) * groups + k],
                device_id=(s, lax.rem(q + 2 * k, chans)), device_id_type=MESH)
            c.start()
            copies.append(c)
        up_copies.append(copies)
        so[0, :, here] = act[:panel]
        so[1, :, here] = act[panel:]
    act_mate = remote(so.at[1 - p], sr, 9, mate)
    act_mate.start()

    loads[4].wait()
    f, a, b, c = lattice(0.0, lat)
    wf = wv[...].astype(f32) + MOST
    key = (wf[0:1] * SIDE + wf[1:2]) * SIDE + wf[2:3]
    hit = (key == f).astype(f32) + ((2.0 * HALF - key) == f).astype(f32)
    times = jnp.sum(hit, axis=1, keepdims=True)
    qa = a * (2.0 * math.pi / n)
    qb = b * (2.0 * math.pi / BLK_DEV)
    qc = c * (2.0 * math.pi)
    k2 = qa * qa + qb * qb + qc * qc
    raw = jnp.exp(-k2 / 2000.0) / (k2 + 100.0)
    norm = jnp.sum(times * raw * raw, axis=0, keepdims=True)
    weight = times * raw * lax.rsqrt(norm) * math.sqrt(3.0 / (n * slots))
    weight = jnp.concatenate([weight, weight], 0)

    for half in range(PARTS):
        for c in up_copies[half]:
            c.wait_recv()
        uh, ul = halves(ug[half].reshape(groups * pair, part_i))
        two = dot(fh[...], jnp.concatenate([uh, ul], 1))
        a, b = halves(two[:, :part_i] + two[:, part_i:] + dot(fl[...], uh))
        a = jnp.concatenate([a[r * pair:(r + 1) * pair] for r in range(NRAD)], 1)
        b = jnp.concatenate([b[r * pair:(r + 1) * pair] for r in range(NRAD)], 1)
        out = dot(jnp.concatenate([a, b], 0), gh[half])
        out = out[:pair] + out[pair:] + dot(a, gl[half])
        if half == 0:
            re[...] = out
        else:
            re[...] += out
    ret_mates = {}
    for layer in (0, 2, 1):
        for blk in range(BLK_DEV):
            w = layer * BLK_DEV + blk
            acc = jnp.where(chosen[0] == w, re[:, :cap], 0.0)
            for e in range(1, NB):
                acc = acc + jnp.where(chosen[e] == w, re[:, e * cap:(e + 1) * cap], 0.0)
            wo[layer, blk] = acc[:panel]
            wp[layer, blk] = acc[panel:]
        ret_mates[layer] = remote(wp.at[layer], rw.at[layer], 10 + layer, mate)
        ret_mates[layer].start()
    ret_up = remote(rt.at[1], hb.at[0], 13, nxt)
    ret_dn = remote(rt.at[0], hb.at[1], 14, prv)
    ret_mates[0].wait_recv()
    rt[0] = wo[0] + rw[0]
    ret_dn.start()
    ret_mates[2].wait_recv()
    rt[1] = wo[2] + rw[2]
    ret_up.start()

    def wait_gather(k, carry):
        gather_copy(k).wait_recv()
        return carry

    lax.fori_loop(1, n, wait_gather, 0)
    sh, sl = halves((sg[...].reshape(rows_all, pair) * weight).T)
    two = dot(jnp.concatenate([sh, sl], 0), th[...])
    far_part = two[:pair] + two[pair:] + dot(sh, tl[...])
    act_mate.wait_recv()
    mine, other = so[p], sr[...]
    first = jnp.where(p == 0, mine, other)
    second = jnp.where(p == 0, other, mine)
    upd[...] = live * (fm + jnp.concatenate([first, second], 1) + far_part[:panel])
    ret_mates[1].wait_recv()
    part = cmask + far_part[panel:] + jnp.concatenate([wo[1, b] + rw[1, b] for b in range(BLK_DEV)], 1)
    ret_up.wait_recv()
    ret_dn.wait_recv()
    grad[...] = live * (part + jnp.concatenate([hb[0, b] + hb[1, b] for b in range(BLK_DEV)], 1))

    for c in (pos_up, pos_dn, feat_up, feat_dn, feat_mate, fwd_lo, fwd_hi, filt_mate, cot_mate,
              act_mate, *ret_mates.values(), ret_up, ret_dn, *sum(pre_copies, []), *sum(up_copies, [])):
        c.wait_send()

    def drain(k, carry):
        reduce_copy(k).wait_send()
        gather_copy(k).wait_send()
        return carry

    lax.fori_loop(1, n, drain, 0)


def shards(n, chans, features, positions, counts, neighbours, wavevectors, filters, cotangent):
    panel, slots = features.shape
    cap = slots // BLK_DEV
    pair = 2 * panel
    groups = chans // 2
    piece = -(-(-(-2 * HALF // n)) // 8) * 8
    while (n * piece) % 32:
        piece += 8
    rows = n * piece
    part_i = cap // PARTS
    vm = pltpu.VMEM
    sm = pltpu.SMEM
    scratch = [
        vm(features.shape, f32),
        vm(positions.shape, f32),
        sm(counts.shape, jnp.int32),
        sm(neighbours.shape, jnp.int32),
        vm(wavevectors.shape, jnp.int32),
        vm(filters.shape, f32),
        vm(cotangent.shape, f32),
        vm((3, 2, panel, slots), f32),
        vm((3, BLK_DEV, 8, cap), f32),
        vm((cap, 8), f32),
        vm(filters.shape, f32),
        vm((NRAD * pair, groups * pair), bf16),
        vm((NRAD * pair, groups * pair), bf16),
        vm((BLK_DEV, panel, cap), f32),
        vm((2, panel, cap), f32),
        vm((PARTS, NRAD * part_i, NB * cap), bf16),
        vm((PARTS, NRAD * part_i, NB * cap), bf16),
        vm((NB * cap, 2 * pair), bf16),
        vm((3 * BLK_DEV, cap, 2 * pair), bf16),
        vm((rows, slots), bf16),
        vm((rows, slots), bf16),
        vm((n, piece, pair), f32),
        vm((n, piece, pair), f32),
        vm((n, piece, pair), f32),
        vm((PARTS, groups, part_i, pair), f32),
        vm((PARTS, max(groups - 1, 1), part_i, pair), f32),
        vm((PARTS, groups, pair, part_i), f32),
        vm((2, panel, cap), f32),
        vm((panel, cap), f32),
        vm((pair, NB * cap), f32),
        vm((3, BLK_DEV, panel, cap), f32),
        vm((3, BLK_DEV, panel, cap), f32),
        vm((3, BLK_DEV, panel, cap), f32),
        vm((2, BLK_DEV, panel, cap), f32),
        vm((2, BLK_DEV, panel, cap), f32),
        pltpu.SemaphoreType.DMA((7,)),
        pltpu.SemaphoreType.DMA((16 + 2 * PARTS * groups,)),
        pltpu.SemaphoreType.DMA((16 + 2 * PARTS * groups,)),
        pltpu.SemaphoreType.DMA((n,)),
        pltpu.SemaphoreType.DMA((n,)),
        pltpu.SemaphoreType.DMA((n,)),
        pltpu.SemaphoreType.DMA((n,)),
    ]
    whole = pl.BlockSpec(memory_space=pltpu.VMEM)
    anywhere = pl.BlockSpec(memory_space=pl.ANY)
    out = jax.ShapeDtypeStruct((panel, slots), f32)
    return pl.pallas_call(
        functools.partial(kernel, n, chans),
        out_shape=(out, out),
        in_specs=[anywhere] * 7,
        out_specs=(whole, whole),
        scratch_shapes=scratch,
        compiler_params=pltpu.CompilerParams(
            collective_id=0, has_side_effects=True, vmem_limit_bytes=60 * 1024 * 1024),
    )(features, positions, counts, neighbours, wavevectors, filters, cotangent)


def solution(mesh):
    return jax.shard_map(
        functools.partial(shards, mesh.shape["space"], mesh.shape["chan"]),
        mesh=mesh,
        in_specs=(
            P("chan", "space"),
            P(None, "space"),
            P("space"),
            P("space", None),
            P(),
            P(None, "chan", None),
            P("chan", "space"),
        ),
        out_specs=(P("chan", "space"), P("chan", "space")),
        check_vma=False,
    )
```

```python
import functools
import math

import jax
import jax.numpy as jnp
from jax import lax
from jax.experimental import pallas as pl
from jax.experimental.pallas import tpu as pltpu
from jax.sharding import PartitionSpec as P

NRAD = 8
NB = 4
BLK_DEV = 2
PARTS = 2
MOST = 4
SIDE = 2 * MOST + 1
HALF = (SIDE**3 - 1) // 2
MESH = pl.DeviceIdType.MESH
f32 = jnp.float32
bf16 = jnp.bfloat16


def halves(x):
    high = x.astype(bf16)
    return high, (x - high.astype(f32)).astype(bf16)


def dot(a, b):
    return jnp.dot(a, b, preferred_element_type=f32)


def dot_nt(a, b):
    return lax.dot_general(a, b, (((1,), (1,)), ((), ())), preferred_element_type=f32)


def turn_cos_sin(p):
    r = (p - jnp.floor(p + 0.5)) * math.pi
    s2 = r * r
    s = 1.0 / 6227020800.0
    for n in (-1.0 / 39916800.0, 1.0 / 362880.0, -1.0 / 5040.0, 1.0 / 120.0, -1.0 / 6.0, 1.0):
        s = s * s2 + n
    s = s * r
    c = 1.0 / 479001600.0
    for n in (-1.0 / 3628800.0, 1.0 / 40320.0, -1.0 / 720.0, 1.0 / 24.0, -0.5, 1.0):
        c = c * s2 + n
    return 1.0 - 2.0 * s * s, 2.0 * s * c


def lattice(first, rows):
    f = lax.broadcasted_iota(jnp.int32, (rows, 1), 0).astype(f32) + (first + HALF + 1.0)
    a = jnp.floor((f + 0.5) * (1.0 / (SIDE * SIDE)))
    rest = f - a * (SIDE * SIDE)
    b = jnp.floor((rest + 0.5) * (1.0 / SIDE))
    c = rest - b * SIDE
    return f, a - MOST, b - MOST, c - MOST


def kernel(n, chans, feat_in, pos_in, counts_in, nbr_in, wv_in, filt_in, cot_in, upd, grad, live_out,
           feat, pos, counts, nbr, wv, filt, cot,
           f6, p6, pt, fx, fh, fl, cm, c2, gh, gl, mts, mt, th, tl, ss, rb, sg, ps, rx, ug, so, sr,
           re, wo, wp, rw, rt, hb, load_s, misc_s, misc_r, red_s, red_r, gat_s, gat_r):
    loads = [
        pltpu.make_async_copy(a, b, load_s.at[i])
        for i, (a, b) in enumerate(zip(
            (feat_in, pos_in, counts_in, nbr_in, wv_in, filt_in, cot_in),
            (feat, pos, counts, nbr, wv, filt, cot)))
    ]
    for c in loads:
        c.start()
    panel, slots = feat.shape
    cap = slots // BLK_DEV
    rows_all = th.shape[0]
    lat = rows_all // 2
    piece = ss.shape[1]
    pair = 2 * panel
    groups = chans // 2
    s = lax.axis_index("space")
    q = lax.axis_index("chan")
    p = lax.rem(q, 2)
    h = lax.div(q, 2)
    mate = (s, q + 1 - 2 * p)
    nxt = (lax.rem(s + 1, n), q)
    prv = (lax.rem(s + n - 1, n), q)

    def remote(src, dst, at, dev):
        return pltpu.make_async_remote_copy(
            src_ref=src, dst_ref=dst, send_sem=misc_s.at[at], recv_sem=misc_r.at[at],
            device_id=dev, device_id_type=MESH)

    barrier = pltpu.get_barrier_semaphore()

    def greet(k, carry):
        pl.semaphore_signal(barrier, inc=1, device_id=(lax.rem(s + k, n), q), device_id_type=MESH)
        return carry

    lax.fori_loop(1, n, greet, 0)
    pl.semaphore_signal(barrier, inc=1, device_id=mate, device_id_type=MESH)
    for k in range(1, groups):
        pl.semaphore_signal(barrier, inc=1, device_id=(s, lax.rem(q + 2 * k, chans)), device_id_type=MESH)

    for at in (0, 1, 2, 6):
        loads[at].wait()
    lane = lax.broadcasted_iota(jnp.int32, (1, slots), 1)
    bound = jnp.where(lane < cap, counts[0], counts[1] + cap)
    live = (lane < bound).astype(f32)
    fm = feat[...] * live
    cmask = cot[...] * live
    f6[1, 0] = fm
    for b in range(BLK_DEV):
        cm[b] = cmask[:, b * cap:(b + 1) * cap]
    p6[1] = jnp.zeros(p6.shape[1:], f32)
    for b in range(BLK_DEV):
        p6[1, b, 0:3, :] = pos[:, b * cap:(b + 1) * cap]

    pl.semaphore_wait(barrier, n - 1 + 1 + groups - 1)

    pos_up = remote(p6.at[1], p6.at[0], 0, nxt)
    pos_dn = remote(p6.at[1], p6.at[2], 1, prv)
    feat_up = remote(f6.at[1, 0], f6.at[0, 0], 2, nxt)
    feat_dn = remote(f6.at[1, 0], f6.at[2, 0], 3, prv)
    feat_mate = remote(f6.at[1, 0], f6.at[1, 1], 4, mate)
    fwd_lo = remote(f6.at[0, 0], f6.at[0, 1], 5, mate)
    fwd_hi = remote(f6.at[2, 0], f6.at[2, 1], 6, mate)
    filt_mate = remote(filt_in, fx, 7, mate)
    cot_mate = remote(cm.at[1 - p], c2.at[p], 8, mate)
    for c in (pos_up, pos_dn, feat_up, feat_dn, feat_mate, filt_mate, cot_mate):
        c.start()
    c2[p] = cm[p]

    chunk = 16
    layer_x = s.astype(f32)
    xs = (pos[0:1, :] + layer_x) * (1.0 / n)
    ys = pos[1:2, :] * (1.0 / BLK_DEV)
    zs = pos[2:3, :]

    def table(i, carry):
        at = pl.multiple_of(i * chunk, chunk)
        _, a, b, c = lattice((i * chunk).astype(f32), chunk)
        cosv, sinv = turn_cos_sin(a * xs + b * ys + c * zs)
        ch, cl = halves(cosv)
        sh, sl = halves(sinv)
        th[pl.ds(at, chunk), :] = ch
        tl[pl.ds(at, chunk), :] = cl
        th[pl.ds(lat + at, chunk), :] = sh
        tl[pl.ds(lat + at, chunk), :] = sl
        return carry

    lax.fori_loop(0, lat // chunk, table, 0)
    vh, vl = halves(jnp.concatenate([fm, cmask], 0))
    two = dot_nt(th[...], jnp.concatenate([vh, vl], 0))
    full = two[:, :pair] + two[:, pair:] + dot_nt(tl[...], vh)
    ss[...] = full.reshape(n, piece, pair)

    def reduce_copy(k):
        return pltpu.make_async_remote_copy(
            src_ref=ss.at[lax.rem(s + k, n)], dst_ref=rb.at[s], send_sem=red_s.at[k],
            recv_sem=red_r.at[k], device_id=(lax.rem(s + k, n), q), device_id_type=MESH)

    def start_reduce(k, carry):
        reduce_copy(k).start()
        return carry

    lax.fori_loop(1, n, start_reduce, 0)

    pos_up.wait_recv()
    pos_dn.wait_recv()
    pt[...] = p6[1, p].T
    loads[3].wait()
    step = 16
    part_i = cap // PARTS
    chosen = [nbr[p, e] for e in range(NB)]

    for half in range(PARTS):
        def radial(i, carry):
            at = pl.multiple_of(i * step, step)
            own = pt[pl.ds(half * part_i + at, step), :]
            for e in range(NB):
                w = chosen[e]
                far = p6[lax.div(w, BLK_DEV), lax.rem(w, BLK_DEV)]
                offset = (lax.div(w, BLK_DEV) - 1).astype(f32)
                dx = own[:, 0:1] - (far[0:1, :] + offset)
                dy = own[:, 1:2] - far[1:2, :]
                dz = own[:, 2:3] - far[2:3, :]
                sq = jnp.minimum(dx * dx + dy * dy + dz * dz, 1.0)
                left = 1.0 - sq
                u = NRAD * jnp.sqrt(sq) - 0.5
                t = jnp.exp(u)
                g = jnp.exp(-0.5 * u * u) * (0.3 * left * left)
                for r in range(NRAD):
                    if r:
                        g = g * (t * math.exp(0.5 - r))
                    a, b = halves(g)
                    gh[half, pl.ds(r * part_i + at, step), e * cap:(e + 1) * cap] = a
                    gl[half, pl.ds(r * part_i + at, step), e * cap:(e + 1) * cap] = b
            return carry

        lax.fori_loop(0, part_i // step, radial, 0)
        if half == 0:
            feat_up.wait_recv()
            fwd_lo.start()
            feat_dn.wait_recv()
            fwd_hi.start()

    feat_mate.wait_recv()
    fwd_lo.wait_recv()
    fwd_hi.wait_recv()
    for layer in range(3):
        both = jnp.concatenate([f6[layer, 0], f6[layer, 1]], 0)
        for b in range(BLK_DEV):
            a, c = halves(both[:, b * cap:(b + 1) * cap].T)
            mt[layer * BLK_DEV + b] = jnp.concatenate([a, c], 1)
    for e in range(NB):
        mts[e * cap:(e + 1) * cap, :] = mt[chosen[e]]
    filt_mate.wait_recv()
    loads[5].wait()
    for r in range(NRAD):
        for i, src in enumerate((filt, fx)):
            a, b = halves(src[r])
            at = r * pair + i * panel
            fh[at:at + panel, :] = a
            fl[at:at + panel, :] = b

    pre_copies = []
    for half in range(PARTS):
        two = dot(gh[half], mts[...])
        sums = two[:, :pair] + two[:, pair:] + dot(gl[half], mts[:, :pair])
        a, b = halves(sums)
        total = None
        for r in range(NRAD):
            here = slice(r * part_i, (r + 1) * part_i)
            wh, wl = fh[r * pair:(r + 1) * pair, :], fl[r * pair:(r + 1) * pair, :]
            term = dot(jnp.concatenate([a[here], b[here]], 1), jnp.concatenate([wh, wh], 0)) + dot(a[here], wl)
            total = term if r == 0 else total + term
        for k in range(groups):
            ps[half, k] = total[:, k * pair:(k + 1) * pair]
        copies = []
        for k in range(1, groups):
            c = remote(ps.at[half, lax.rem(h + k, groups)], rx.at[half, k - 1], 16 + half * groups + k,
                       (s, lax.rem(q + 2 * k, chans)))
            c.start()
            copies.append(c)
        pre_copies.append(copies)

    cot_mate.wait_recv()
    up_copies = []
    for half in range(PARTS):
        here = slice(half * part_i, (half + 1) * part_i)
        for c in pre_copies[half]:
            c.wait_recv()
        acc = ps[half, h]
        for k in range(1, groups):
            acc = acc + rx[half, k - 1]
        pre = acc.T
        sigma = 1.0 / (1.0 + jnp.exp(-pre))
        act = pre * sigma
        ug[half, h] = jnp.concatenate([c2[0, :, here], c2[1, :, here]], 0) * sigma * (1.0 + pre * (1.0 - sigma))
        copies = []
        for k in range(1, groups):
            c = pltpu.make_async_remote_copy(
                src_ref=ug.at[half, h], dst_ref=ug.at[half, h], send_sem=misc_s.at[16 + (PARTS + half) * groups + k],
                recv_sem=misc_r.at[16 + (PARTS + half) * groups + k],
                device_id=(s, lax.rem(q + 2 * k, chans)), device_id_type=MESH)
            c.start()
            copies.append(c)
        up_copies.append(copies)
        so[0, :, here] = act[:panel]
        so[1, :, here] = act[panel:]
    act_mate = remote(so.at[1 - p], sr, 9, mate)
    act_mate.start()

    def wait_reduce(k, carry):
        reduce_copy(k).wait_recv()
        return carry

    lax.fori_loop(1, n, wait_reduce, 0)
    rb[s] = ss[s]

    def add_up(k, acc):
        return acc + rb[k]

    sg[s] = lax.fori_loop(0, n, add_up, jnp.zeros((piece, pair), f32))

    def gather_copy(k):
        return pltpu.make_async_remote_copy(
            src_ref=sg.at[s], dst_ref=sg.at[s], send_sem=gat_s.at[k],
            recv_sem=gat_r.at[k], device_id=(lax.rem(s + k, n), q), device_id_type=MESH)

    def start_gather(k, carry):
        gather_copy(k).start()
        return carry

    lax.fori_loop(1, n, start_gather, 0)

    loads[4].wait()
    f, a, b, c = lattice(0.0, lat)
    wf = wv[...].astype(f32) + MOST
    key = (wf[0:1] * SIDE + wf[1:2]) * SIDE + wf[2:3]
    hit = (key == f).astype(f32) + ((2.0 * HALF - key) == f).astype(f32)
    times = jnp.sum(hit, axis=1, keepdims=True)
    qa = a * (2.0 * math.pi / n)
    qb = b * (2.0 * math.pi / BLK_DEV)
    qc = c * (2.0 * math.pi)
    k2 = qa * qa + qb * qb + qc * qc
    raw = jnp.exp(-k2 / 2000.0) / (k2 + 100.0)
    norm = jnp.sum(times * raw * raw, axis=0, keepdims=True)
    weight = times * raw * lax.rsqrt(norm) * math.sqrt(3.0 / (n * slots))
    weight = jnp.concatenate([weight, weight], 0)

    pair_cots = []
    for half in range(PARTS):
        for c in up_copies[half]:
            c.wait_recv()
        uh, ul = halves(ug[half].reshape(groups * pair, part_i))
        two = dot(fh[...], jnp.concatenate([uh, ul], 1))
        a, b = halves(two[:, :part_i] + two[:, part_i:] + dot(fl[...], uh))
        a = jnp.concatenate([a[r * pair:(r + 1) * pair] for r in range(NRAD)], 1)
        b = jnp.concatenate([b[r * pair:(r + 1) * pair] for r in range(NRAD)], 1)
        both = jnp.concatenate([a, b], 0)
        pair_cots.append((a, both))
        out = dot(both, gh[half, :, cap:])
        out = out[:pair] + out[pair:] + dot(a, gl[half, :, cap:])
        if half == 0:
            re[:, cap:] = out
        else:
            re[:, cap:] += out
    ret_mates = {}

    def window_sums(layer, entries):
        for blk in range(BLK_DEV):
            w = layer * BLK_DEV + blk
            acc = None
            for e in entries:
                term = jnp.where(chosen[e] == w, re[:, e * cap:(e + 1) * cap], 0.0)
                acc = term if acc is None else acc + term
            wo[layer, blk] = acc[:panel]
            wp[layer, blk] = acc[panel:]
        ret_mates[layer] = remote(wp.at[layer], rw.at[layer], 10 + layer, mate)
        ret_mates[layer].start()

    window_sums(0, range(1, NB))
    window_sums(2, range(1, NB))
    out = None
    for half in range(PARTS):
        a, both = pair_cots[half]
        term = dot(both, gh[half, :, :cap])
        term = term[:pair] + term[pair:] + dot(a, gl[half, :, :cap])
        out = term if half == 0 else out + term
    re[:, :cap] = out
    ret_up = remote(rt.at[1], hb.at[0], 13, nxt)
    ret_dn = remote(rt.at[0], hb.at[1], 14, prv)
    ret_mates[0].wait_recv()
    rt[0] = wo[0] + rw[0]
    ret_dn.start()
    ret_mates[2].wait_recv()
    rt[1] = wo[2] + rw[2]
    ret_up.start()
    window_sums(1, range(NB))

    def wait_gather(k, carry):
        gather_copy(k).wait_recv()
        return carry

    lax.fori_loop(1, n, wait_gather, 0)
    sh, sl = halves((sg[...].reshape(rows_all, pair) * weight).T)
    two = dot(jnp.concatenate([sh, sl], 0), th[...])
    far_part = two[:pair] + two[pair:] + dot(sh, tl[...])
    act_mate.wait_recv()
    mine, other = so[p], sr[...]
    first = jnp.where(p == 0, mine, other)
    second = jnp.where(p == 0, other, mine)
    live_out[...] = jnp.broadcast_to(live, live_out.shape)
    upd[...] = (fm + jnp.concatenate([first, second], 1) + far_part[:panel])
    ret_mates[1].wait_recv()
    part = cmask + far_part[panel:] + jnp.concatenate([wo[1, b] + rw[1, b] for b in range(BLK_DEV)], 1)
    ret_up.wait_recv()
    ret_dn.wait_recv()
    grad[...] = (part + jnp.concatenate([hb[0, b] + hb[1, b] for b in range(BLK_DEV)], 1))

    for c in (pos_up, pos_dn, feat_up, feat_dn, feat_mate, fwd_lo, fwd_hi, filt_mate, cot_mate,
              act_mate, *ret_mates.values(), ret_up, ret_dn, *sum(pre_copies, []), *sum(up_copies, [])):
        c.wait_send()

    def drain(k, carry):
        reduce_copy(k).wait_send()
        gather_copy(k).wait_send()
        return carry

    lax.fori_loop(1, n, drain, 0)


def shards(n, chans, features, positions, counts, neighbours, wavevectors, filters, cotangent):
    panel, slots = features.shape
    cap = slots // BLK_DEV
    pair = 2 * panel
    groups = chans // 2
    piece = -(-(-(-2 * HALF // n)) // 8) * 8
    while (n * piece) % 32:
        piece += 8
    rows = n * piece
    part_i = cap // PARTS
    vm = pltpu.VMEM
    sm = pltpu.SMEM
    scratch = [
        vm(features.shape, f32),
        vm(positions.shape, f32),
        sm(counts.shape, jnp.int32),
        sm(neighbours.shape, jnp.int32),
        vm(wavevectors.shape, jnp.int32),
        vm(filters.shape, f32),
        vm(cotangent.shape, f32),
        vm((3, 2, panel, slots), f32),
        vm((3, BLK_DEV, 8, cap), f32),
        vm((cap, 8), f32),
        vm(filters.shape, f32),
        vm((NRAD * pair, groups * pair), bf16),
        vm((NRAD * pair, groups * pair), bf16),
        vm((BLK_DEV, panel, cap), f32),
        vm((2, panel, cap), f32),
        vm((PARTS, NRAD * part_i, NB * cap), bf16),
        vm((PARTS, NRAD * part_i, NB * cap), bf16),
        vm((NB * cap, 2 * pair), bf16),
        vm((3 * BLK_DEV, cap, 2 * pair), bf16),
        vm((rows, slots), bf16),
        vm((rows, slots), bf16),
        vm((n, piece, pair), f32),
        vm((n, piece, pair), f32),
        vm((n, piece, pair), f32),
        vm((PARTS, groups, part_i, pair), f32),
        vm((PARTS, max(groups - 1, 1), part_i, pair), f32),
        vm((PARTS, groups, pair, part_i), f32),
        vm((2, panel, cap), f32),
        vm((panel, cap), f32),
        vm((pair, NB * cap), f32),
        vm((3, BLK_DEV, panel, cap), f32),
        vm((3, BLK_DEV, panel, cap), f32),
        vm((3, BLK_DEV, panel, cap), f32),
        vm((2, BLK_DEV, panel, cap), f32),
        vm((2, BLK_DEV, panel, cap), f32),
        pltpu.SemaphoreType.DMA((7,)),
        pltpu.SemaphoreType.DMA((16 + 2 * PARTS * groups,)),
        pltpu.SemaphoreType.DMA((16 + 2 * PARTS * groups,)),
        pltpu.SemaphoreType.DMA((n,)),
        pltpu.SemaphoreType.DMA((n,)),
        pltpu.SemaphoreType.DMA((n,)),
        pltpu.SemaphoreType.DMA((n,)),
    ]
    whole = pl.BlockSpec(memory_space=pltpu.VMEM)
    anywhere = pl.BlockSpec(memory_space=pl.ANY)
    out = jax.ShapeDtypeStruct((panel, slots), f32)
    upd, grad, live = pl.pallas_call(
        functools.partial(kernel, n, chans),
        out_shape=(out, out, out),
        in_specs=[anywhere] * 7,
        out_specs=(whole, whole, whole),
        scratch_shapes=scratch,
        compiler_params=pltpu.CompilerParams(
            collective_id=0, has_side_effects=True, vmem_limit_bytes=60 * 1024 * 1024),
    )(features, positions, counts, neighbours, wavevectors, filters, cotangent)
    return upd * live, grad * live


def solution(mesh):
    return jax.shard_map(
        functools.partial(shards, mesh.shape["space"], mesh.shape["chan"]),
        mesh=mesh,
        in_specs=(
            P("chan", "space"),
            P(None, "space"),
            P("space"),
            P("space", None),
            P(),
            P(None, "chan", None),
            P("chan", "space"),
        ),
        out_specs=(P("chan", "space"), P("chan", "space")),
        check_vma=False,
    )
```

```python
import functools
import math

import jax
import jax.numpy as jnp
from jax import lax
from jax.experimental import pallas as pl
from jax.experimental.pallas import tpu as pltpu
from jax.sharding import PartitionSpec as P

NRAD = 8
NB = 4
BLK_DEV = 2
PARTS = 2
MOST = 4
SIDE = 2 * MOST + 1
HALF = (SIDE**3 - 1) // 2
MESH = pl.DeviceIdType.MESH
f32 = jnp.float32
bf16 = jnp.bfloat16


def halves(x):
    high = x.astype(bf16)
    return high, (x - high.astype(f32)).astype(bf16)


def dot(a, b):
    return jnp.dot(a, b, preferred_element_type=f32)


def dot_nt(a, b):
    return lax.dot_general(a, b, (((1,), (1,)), ((), ())), preferred_element_type=f32)


def turn_cos_sin(p):
    r = (p - jnp.floor(p + 0.5)) * math.pi
    s2 = r * r
    s = 1.0 / 6227020800.0
    for n in (-1.0 / 39916800.0, 1.0 / 362880.0, -1.0 / 5040.0, 1.0 / 120.0, -1.0 / 6.0, 1.0):
        s = s * s2 + n
    s = s * r
    c = 1.0 / 479001600.0
    for n in (-1.0 / 3628800.0, 1.0 / 40320.0, -1.0 / 720.0, 1.0 / 24.0, -0.5, 1.0):
        c = c * s2 + n
    return 1.0 - 2.0 * s * s, 2.0 * s * c


def lattice(first, rows):
    f = lax.broadcasted_iota(jnp.int32, (rows, 1), 0).astype(f32) + (first + HALF + 1.0)
    a = jnp.floor((f + 0.5) * (1.0 / (SIDE * SIDE)))
    rest = f - a * (SIDE * SIDE)
    b = jnp.floor((rest + 0.5) * (1.0 / SIDE))
    c = rest - b * SIDE
    return f, a - MOST, b - MOST, c - MOST


def kernel(n, chans, feat_in, pos_in, counts_in, nbr_in, wv_in, filt_in, cot_in, upd, grad, live_out,
           feat, pos, counts, nbr, wv, filt, cot,
           f6, p6, pt, fx, fh, fl, cm, c2, gh, gl, mts, mt, vs, th, tl, ss, rb, sg, ps, rx, ug, so, sr,
           re, wo, wp, rw, rt, hb, load_s, misc_s, misc_r, red_s, red_r, gat_s, gat_r):
    loads = [
        pltpu.make_async_copy(a, b, load_s.at[i])
        for i, (a, b) in enumerate(zip(
            (feat_in, pos_in, counts_in, nbr_in, wv_in, filt_in, cot_in),
            (feat, pos, counts, nbr, wv, filt, cot)))
    ]
    for c in loads:
        c.start()
    panel, slots = feat.shape
    cap = slots // BLK_DEV
    piece = ss.shape[1]
    grain = piece // 2
    rows_all = n * piece
    pair = 2 * panel
    groups = chans // 2
    s = lax.axis_index("space")
    q = lax.axis_index("chan")
    p = lax.rem(q, 2)
    h = lax.div(q, 2)
    mate = (s, q + 1 - 2 * p)
    nxt = (lax.rem(s + 1, n), q)
    prv = (lax.rem(s + n - 1, n), q)

    def remote(src, dst, at, dev):
        return pltpu.make_async_remote_copy(
            src_ref=src, dst_ref=dst, send_sem=misc_s.at[at], recv_sem=misc_r.at[at],
            device_id=dev, device_id_type=MESH)

    barrier = pltpu.get_barrier_semaphore()

    def greet(k, carry):
        pl.semaphore_signal(barrier, inc=1, device_id=(lax.rem(s + k, n), q), device_id_type=MESH)
        return carry

    lax.fori_loop(1, n, greet, 0)
    pl.semaphore_signal(barrier, inc=1, device_id=mate, device_id_type=MESH)
    for k in range(1, groups):
        pl.semaphore_signal(barrier, inc=1, device_id=(s, lax.rem(q + 2 * k, chans)), device_id_type=MESH)

    for at in (0, 1, 2, 6):
        loads[at].wait()
    lane = lax.broadcasted_iota(jnp.int32, (1, slots), 1)
    bound = jnp.where(lane < cap, counts[0], counts[1] + cap)
    live = (lane < bound).astype(f32)
    fm = feat[...] * live
    cmask = cot[...] * live
    f6[1, 0] = fm
    for b in range(BLK_DEV):
        cm[b] = cmask[:, b * cap:(b + 1) * cap]
    p6[1] = jnp.zeros(p6.shape[1:], f32)
    for b in range(BLK_DEV):
        p6[1, b, 0:3, :] = pos[:, b * cap:(b + 1) * cap]

    pl.semaphore_wait(barrier, n - 1 + 1 + groups - 1)

    pos_up = remote(p6.at[1], p6.at[0], 0, nxt)
    pos_dn = remote(p6.at[1], p6.at[2], 1, prv)
    feat_up = remote(f6.at[1, 0], f6.at[0, 0], 2, nxt)
    feat_dn = remote(f6.at[1, 0], f6.at[2, 0], 3, prv)
    feat_mate = remote(f6.at[1, 0], f6.at[1, 1], 4, mate)
    fwd_lo = remote(f6.at[0, 0], f6.at[0, 1], 5, mate)
    fwd_hi = remote(f6.at[2, 0], f6.at[2, 1], 6, mate)
    filt_mate = remote(filt_in, fx, 7, mate)
    cot_mate = remote(cm.at[1 - p], c2.at[p], 8, mate)
    for c in (pos_up, pos_dn, feat_up, feat_dn, feat_mate, filt_mate, cot_mate):
        c.start()
    c2[p] = cm[p]

    chunk = 16
    layer_x = s.astype(f32)
    xs = (pos[0:1, :] + layer_x) * (1.0 / n)
    ys = pos[1:2, :] * (1.0 / BLK_DEV)
    zs = pos[2:3, :]

    def reduce_copy(k):
        return pltpu.make_async_remote_copy(
            src_ref=ss.at[lax.rem(s + k, n)], dst_ref=rb.at[s], send_sem=red_s.at[k],
            recv_sem=red_r.at[k], device_id=(lax.rem(s + k, n), q), device_id_type=MESH)

    vh, vl = halves(jnp.concatenate([fm, cmask], 0))
    vs[...] = jnp.concatenate([vh, vl], 0)

    def send_piece(k, carry):
        to = lax.rem(s + k, n)
        for at in range(0, grain, chunk):
            _, a, b, c = lattice((to * grain + at).astype(f32), chunk)
            cosv, sinv = turn_cos_sin(a * xs + b * ys + c * zs)
            th[to, at:at + chunk, :], tl[to, at:at + chunk, :] = halves(cosv)
            th[to, grain + at:grain + at + chunk, :], tl[to, grain + at:grain + at + chunk, :] = halves(sinv)
        two = dot_nt(th[to], vs[...])
        ss[to] = two[:, :pair] + two[:, pair:] + dot_nt(tl[to], vs[:pair, :])

        @pl.when(k < n)
        def _():
            reduce_copy(k).start()

        return carry

    lax.fori_loop(1, n + 1, send_piece, 0)

    pos_up.wait_recv()
    pos_dn.wait_recv()
    pt[...] = p6[1, p].T
    loads[3].wait()
    step = 16
    part_i = cap // PARTS
    chosen = [nbr[p, e] for e in range(NB)]

    for half in range(PARTS):
        def radial(i, carry):
            at = pl.multiple_of(i * step, step)
            own = pt[pl.ds(half * part_i + at, step), :]
            for e in range(NB):
                w = chosen[e]
                far = p6[lax.div(w, BLK_DEV), lax.rem(w, BLK_DEV)]
                offset = (lax.div(w, BLK_DEV) - 1).astype(f32)
                dx = own[:, 0:1] - (far[0:1, :] + offset)
                dy = own[:, 1:2] - far[1:2, :]
                dz = own[:, 2:3] - far[2:3, :]
                sq = jnp.minimum(dx * dx + dy * dy + dz * dz, 1.0)
                left = 1.0 - sq
                u = NRAD * jnp.sqrt(sq) - 0.5
                t = jnp.exp(u)
                g = jnp.exp(-0.5 * u * u) * (0.3 * left * left)
                for r in range(NRAD):
                    if r:
                        g = g * (t * math.exp(0.5 - r))
                    a, b = halves(g)
                    gh[half, pl.ds(r * part_i + at, step), e * cap:(e + 1) * cap] = a
                    gl[half, pl.ds(r * part_i + at, step), e * cap:(e + 1) * cap] = b
            return carry

        lax.fori_loop(0, part_i // step, radial, 0)
        if half == 0:
            feat_up.wait_recv()
            fwd_lo.start()
            feat_dn.wait_recv()
            fwd_hi.start()

    feat_mate.wait_recv()
    fwd_lo.wait_recv()
    fwd_hi.wait_recv()
    for layer in range(3):
        both = jnp.concatenate([f6[layer, 0], f6[layer, 1]], 0)
        for b in range(BLK_DEV):
            a, c = halves(both[:, b * cap:(b + 1) * cap].T)
            mt[layer * BLK_DEV + b] = jnp.concatenate([a, c], 1)
    for e in range(NB):
        mts[e * cap:(e + 1) * cap, :] = mt[chosen[e]]
    filt_mate.wait_recv()
    loads[5].wait()
    for r in range(NRAD):
        for i, src in enumerate((filt, fx)):
            a, b = halves(src[r])
            at = r * pair + i * panel
            fh[at:at + panel, :] = a
            fl[at:at + panel, :] = b

    def gather_copy(k):
        return pltpu.make_async_remote_copy(
            src_ref=sg.at[s], dst_ref=sg.at[s], send_sem=gat_s.at[k],
            recv_sem=gat_r.at[k], device_id=(lax.rem(s + k, n), q), device_id_type=MESH)

    def all_gather_start():
        def wait_reduce(k, carry):
            reduce_copy(k).wait_recv()
            return carry

        lax.fori_loop(1, n, wait_reduce, 0)
        rb[s] = ss[s]

        def add_up(k, acc):
            return acc + rb[k]

        sg[s] = lax.fori_loop(0, n, add_up, jnp.zeros((piece, pair), f32))

        def start_gather(k, carry):
            gather_copy(k).start()
            return carry

        lax.fori_loop(1, n, start_gather, 0)

    pre_copies = []
    for half in range(PARTS):
        two = dot(gh[half], mts[...])
        sums = two[:, :pair] + two[:, pair:] + dot(gl[half], mts[:, :pair])
        a, b = halves(sums)
        total = None
        for r in range(NRAD):
            here = slice(r * part_i, (r + 1) * part_i)
            wh, wl = fh[r * pair:(r + 1) * pair, :], fl[r * pair:(r + 1) * pair, :]
            term = dot(jnp.concatenate([a[here], b[here]], 1), jnp.concatenate([wh, wh], 0)) + dot(a[here], wl)
            total = term if r == 0 else total + term
        for k in range(groups):
            ps[half, k] = total[:, k * pair:(k + 1) * pair]
        copies = []
        for k in range(1, groups):
            c = remote(ps.at[half, lax.rem(h + k, groups)], rx.at[half, k - 1], 16 + half * groups + k,
                       (s, lax.rem(q + 2 * k, chans)))
            c.start()
            copies.append(c)
        pre_copies.append(copies)
        if half == 0:
            all_gather_start()

    cot_mate.wait_recv()
    up_copies = []
    for half in range(PARTS):
        here = slice(half * part_i, (half + 1) * part_i)
        for c in pre_copies[half]:
            c.wait_recv()
        acc = ps[half, h]
        for k in range(1, groups):
            acc = acc + rx[half, k - 1]
        pre = acc.T
        sigma = 1.0 / (1.0 + jnp.exp(-pre))
        act = pre * sigma
        ug[half, h] = jnp.concatenate([c2[0, :, here], c2[1, :, here]], 0) * sigma * (1.0 + pre * (1.0 - sigma))
        copies = []
        for k in range(1, groups):
            c = pltpu.make_async_remote_copy(
                src_ref=ug.at[half, h], dst_ref=ug.at[half, h], send_sem=misc_s.at[16 + (PARTS + half) * groups + k],
                recv_sem=misc_r.at[16 + (PARTS + half) * groups + k],
                device_id=(s, lax.rem(q + 2 * k, chans)), device_id_type=MESH)
            c.start()
            copies.append(c)
        up_copies.append(copies)
        so[0, :, here] = act[:panel]
        so[1, :, here] = act[panel:]
    act_mate = remote(so.at[1 - p], sr, 9, mate)
    act_mate.start()

    loads[4].wait()
    f, a, b, c = lattice(0.0, n * grain)
    wf = wv[...].astype(f32) + MOST
    key = (wf[0:1] * SIDE + wf[1:2]) * SIDE + wf[2:3]
    hit = (key == f).astype(f32) + ((2.0 * HALF - key) == f).astype(f32)
    times = jnp.sum(hit, axis=1, keepdims=True)
    qa = a * (2.0 * math.pi / n)
    qb = b * (2.0 * math.pi / BLK_DEV)
    qc = c * (2.0 * math.pi)
    k2 = qa * qa + qb * qb + qc * qc
    raw = jnp.exp(-k2 / 2000.0) / (k2 + 100.0)
    norm = jnp.sum(times * raw * raw, axis=0, keepdims=True)
    weight = times * raw * lax.rsqrt(norm) * math.sqrt(3.0 / (n * slots))
    weight = weight.reshape(n, grain, 1)
    weight = jnp.concatenate([weight, weight], 1).reshape(rows_all, 1)

    pair_cots = []
    for half in range(PARTS):
        for c in up_copies[half]:
            c.wait_recv()
        uh, ul = halves(ug[half].reshape(groups * pair, part_i))
        two = dot(fh[...], jnp.concatenate([uh, ul], 1))
        a, b = halves(two[:, :part_i] + two[:, part_i:] + dot(fl[...], uh))
        a = jnp.concatenate([a[r * pair:(r + 1) * pair] for r in range(NRAD)], 1)
        b = jnp.concatenate([b[r * pair:(r + 1) * pair] for r in range(NRAD)], 1)
        both = jnp.concatenate([a, b], 0)
        pair_cots.append((a, both))
        out = dot(both, gh[half, :, cap:])
        out = out[:pair] + out[pair:] + dot(a, gl[half, :, cap:])
        if half == 0:
            re[:, cap:] = out
        else:
            re[:, cap:] += out
    ret_mates = {}

    def window_sums(layer, entries):
        for blk in range(BLK_DEV):
            w = layer * BLK_DEV + blk
            acc = None
            for e in entries:
                term = jnp.where(chosen[e] == w, re[:, e * cap:(e + 1) * cap], 0.0)
                acc = term if acc is None else acc + term
            wo[layer, blk] = acc[:panel]
            wp[layer, blk] = acc[panel:]
        ret_mates[layer] = remote(wp.at[layer], rw.at[layer], 10 + layer, mate)
        ret_mates[layer].start()

    window_sums(0, range(1, NB))
    window_sums(2, range(1, NB))
    out = None
    for half in range(PARTS):
        a, both = pair_cots[half]
        term = dot(both, gh[half, :, :cap])
        term = term[:pair] + term[pair:] + dot(a, gl[half, :, :cap])
        out = term if half == 0 else out + term
    re[:, :cap] = out
    ret_up = remote(rt.at[1], hb.at[0], 13, nxt)
    ret_dn = remote(rt.at[0], hb.at[1], 14, prv)
    ret_mates[0].wait_recv()
    rt[0] = wo[0] + rw[0]
    ret_dn.start()
    ret_mates[2].wait_recv()
    rt[1] = wo[2] + rw[2]
    ret_up.start()
    window_sums(1, range(NB))

    def wait_gather(k, carry):
        gather_copy(k).wait_recv()
        return carry

    lax.fori_loop(1, n, wait_gather, 0)
    sh, sl = halves((sg[...].reshape(rows_all, pair) * weight).T)
    two = dot(jnp.concatenate([sh, sl], 0), th[...].reshape(rows_all, slots))
    far_part = two[:pair] + two[pair:] + dot(sh, tl[...].reshape(rows_all, slots))
    act_mate.wait_recv()
    mine, other = so[p], sr[...]
    first = jnp.where(p == 0, mine, other)
    second = jnp.where(p == 0, other, mine)
    live_out[...] = jnp.broadcast_to(live, live_out.shape)
    upd[...] = (fm + jnp.concatenate([first, second], 1) + far_part[:panel])
    ret_mates[1].wait_recv()
    part = cmask + far_part[panel:] + jnp.concatenate([wo[1, b] + rw[1, b] for b in range(BLK_DEV)], 1)
    ret_up.wait_recv()
    ret_dn.wait_recv()
    grad[...] = (part + jnp.concatenate([hb[0, b] + hb[1, b] for b in range(BLK_DEV)], 1))

    for c in (pos_up, pos_dn, feat_up, feat_dn, feat_mate, fwd_lo, fwd_hi, filt_mate, cot_mate,
              act_mate, *ret_mates.values(), ret_up, ret_dn, *sum(pre_copies, []), *sum(up_copies, [])):
        c.wait_send()

    def drain(k, carry):
        reduce_copy(k).wait_send()
        gather_copy(k).wait_send()
        return carry

    lax.fori_loop(1, n, drain, 0)


def shards(n, chans, features, positions, counts, neighbours, wavevectors, filters, cotangent):
    panel, slots = features.shape
    cap = slots // BLK_DEV
    pair = 2 * panel
    groups = chans // 2
    piece = -(-(-(-2 * HALF // n)) // 32) * 32
    part_i = cap // PARTS
    vm = pltpu.VMEM
    sm = pltpu.SMEM
    scratch = [
        vm(features.shape, f32),
        vm(positions.shape, f32),
        sm(counts.shape, jnp.int32),
        sm(neighbours.shape, jnp.int32),
        vm(wavevectors.shape, jnp.int32),
        vm(filters.shape, f32),
        vm(cotangent.shape, f32),
        vm((3, 2, panel, slots), f32),
        vm((3, BLK_DEV, 8, cap), f32),
        vm((cap, 8), f32),
        vm(filters.shape, f32),
        vm((NRAD * pair, groups * pair), bf16),
        vm((NRAD * pair, groups * pair), bf16),
        vm((BLK_DEV, panel, cap), f32),
        vm((2, panel, cap), f32),
        vm((PARTS, NRAD * part_i, NB * cap), bf16),
        vm((PARTS, NRAD * part_i, NB * cap), bf16),
        vm((NB * cap, 2 * pair), bf16),
        vm((3 * BLK_DEV, cap, 2 * pair), bf16),
        vm((2 * pair, slots), bf16),
        vm((n, piece, slots), bf16),
        vm((n, piece, slots), bf16),
        vm((n, piece, pair), f32),
        vm((n, piece, pair), f32),
        vm((n, piece, pair), f32),
        vm((PARTS, groups, part_i, pair), f32),
        vm((PARTS, max(groups - 1, 1), part_i, pair), f32),
        vm((PARTS, groups, pair, part_i), f32),
        vm((2, panel, cap), f32),
        vm((panel, cap), f32),
        vm((pair, NB * cap), f32),
        vm((3, BLK_DEV, panel, cap), f32),
        vm((3, BLK_DEV, panel, cap), f32),
        vm((3, BLK_DEV, panel, cap), f32),
        vm((2, BLK_DEV, panel, cap), f32),
        vm((2, BLK_DEV, panel, cap), f32),
        pltpu.SemaphoreType.DMA((7,)),
        pltpu.SemaphoreType.DMA((16 + 2 * PARTS * groups,)),
        pltpu.SemaphoreType.DMA((16 + 2 * PARTS * groups,)),
        pltpu.SemaphoreType.DMA((n,)),
        pltpu.SemaphoreType.DMA((n,)),
        pltpu.SemaphoreType.DMA((n,)),
        pltpu.SemaphoreType.DMA((n,)),
    ]
    whole = pl.BlockSpec(memory_space=pltpu.VMEM)
    anywhere = pl.BlockSpec(memory_space=pl.ANY)
    out = jax.ShapeDtypeStruct((panel, slots), f32)
    upd, grad, live = pl.pallas_call(
        functools.partial(kernel, n, chans),
        out_shape=(out, out, out),
        in_specs=[anywhere] * 7,
        out_specs=(whole, whole, whole),
        scratch_shapes=scratch,
        compiler_params=pltpu.CompilerParams(
            collective_id=0, has_side_effects=True, vmem_limit_bytes=60 * 1024 * 1024),
    )(features, positions, counts, neighbours, wavevectors, filters, cotangent)
    return upd * live, grad * live


def solution(mesh):
    return jax.shard_map(
        functools.partial(shards, mesh.shape["space"], mesh.shape["chan"]),
        mesh=mesh,
        in_specs=(
            P("chan", "space"),
            P(None, "space"),
            P("space"),
            P("space", None),
            P(),
            P(None, "chan", None),
            P("chan", "space"),
        ),
        out_specs=(P("chan", "space"), P("chan", "space")),
        check_vma=False,
    )
```

```python
import functools
import math

import jax
import jax.numpy as jnp
from jax import lax
from jax.experimental import pallas as pl
from jax.experimental.pallas import tpu as pltpu
from jax.sharding import PartitionSpec as P

NRAD = 8
NB = 4
BLK_DEV = 2
PARTS = 2
MOST = 4
SIDE = 2 * MOST + 1
HALF = (SIDE**3 - 1) // 2
MESH = pl.DeviceIdType.MESH
f32 = jnp.float32
bf16 = jnp.bfloat16


def halves(x):
    high = x.astype(bf16)
    return high, (x - high.astype(f32)).astype(bf16)


def dot(a, b):
    return jnp.dot(a, b, preferred_element_type=f32)


def turn_cos_sin(p):
    r = (p - jnp.floor(p + 0.5)) * math.pi
    s2 = r * r
    s = 1.0 / 6227020800.0
    for n in (-1.0 / 39916800.0, 1.0 / 362880.0, -1.0 / 5040.0, 1.0 / 120.0, -1.0 / 6.0, 1.0):
        s = s * s2 + n
    s = s * r
    c = 1.0 / 479001600.0
    for n in (-1.0 / 3628800.0, 1.0 / 40320.0, -1.0 / 720.0, 1.0 / 24.0, -0.5, 1.0):
        c = c * s2 + n
    return 1.0 - 2.0 * s * s, 2.0 * s * c


def lattice(first, rows):
    f = lax.broadcasted_iota(jnp.int32, (rows, 1), 0).astype(f32) + (first + HALF + 1.0)
    a = jnp.floor((f + 0.5) * (1.0 / (SIDE * SIDE)))
    rest = f - a * (SIDE * SIDE)
    b = jnp.floor((rest + 0.5) * (1.0 / SIDE))
    c = rest - b * SIDE
    return f, a - MOST, b - MOST, c - MOST


def kernel(n, chans, feat_in, pos_in, counts_in, nbr_in, wv_in, filt_in, cot_in, upd, grad, live_out,
           feat, pos, counts, nbr, wv, filt, cot,
           f6, p6, pt, fx, fh, fl, cm, c2, gh, gl, mts, mt, vs, th, tl, ss, rb, sg, ps, rx, ug, so, sr,
           re, wo, wp, rw, rt, hb, load_s, misc_s, misc_r, red_s, red_r, gat_s, gat_r):
    loads = [
        pltpu.make_async_copy(a, b, load_s.at[i])
        for i, (a, b) in enumerate(zip(
            (feat_in, pos_in, counts_in, nbr_in, wv_in, filt_in, cot_in),
            (feat, pos, counts, nbr, wv, filt, cot)))
    ]
    for c in loads:
        c.start()
    panel, slots = feat.shape
    cap = slots // BLK_DEV
    piece = ss.shape[1]
    grain = piece // 2
    rows_all = n * piece
    pair = 2 * panel
    groups = chans // 2
    s = lax.axis_index("space")
    q = lax.axis_index("chan")
    p = lax.rem(q, 2)
    h = lax.div(q, 2)
    mate = (s, q + 1 - 2 * p)
    nxt = (lax.rem(s + 1, n), q)
    prv = (lax.rem(s + n - 1, n), q)

    def remote(src, dst, at, dev):
        return pltpu.make_async_remote_copy(
            src_ref=src, dst_ref=dst, send_sem=misc_s.at[at], recv_sem=misc_r.at[at],
            device_id=dev, device_id_type=MESH)

    barrier = pltpu.get_barrier_semaphore()

    def greet(k, carry):
        pl.semaphore_signal(barrier, inc=1, device_id=(lax.rem(s + k, n), q), device_id_type=MESH)
        return carry

    lax.fori_loop(1, n, greet, 0)
    pl.semaphore_signal(barrier, inc=1, device_id=mate, device_id_type=MESH)
    for k in range(1, groups):
        pl.semaphore_signal(barrier, inc=1, device_id=(s, lax.rem(q + 2 * k, chans)), device_id_type=MESH)

    for at in (0, 1, 2, 6):
        loads[at].wait()
    lane = lax.broadcasted_iota(jnp.int32, (1, slots), 1)
    bound = jnp.where(lane < cap, counts[0], counts[1] + cap)
    live = (lane < bound).astype(f32)
    fm = feat[...] * live
    cmask = cot[...] * live
    f6[1, 0] = fm
    for b in range(BLK_DEV):
        cm[b] = cmask[:, b * cap:(b + 1) * cap]
    p6[1] = jnp.zeros(p6.shape[1:], f32)
    for b in range(BLK_DEV):
        p6[1, b, 0:3, :] = pos[:, b * cap:(b + 1) * cap]

    def split_filters(src, i):
        for r in range(NRAD):
            a, b = halves(src[r] * math.exp(-0.5 * r * r))
            at = r * pair + i * panel
            fh[at:at + panel, :] = a
            fl[at:at + panel, :] = b

    loads[5].wait()
    split_filters(filt, 0)
    loads[4].wait()
    f, a, b, c = lattice(0.0, n * grain)
    wf = wv[...].astype(f32) + MOST
    key = (wf[0:1] * SIDE + wf[1:2]) * SIDE + wf[2:3]
    hit = (key == f).astype(f32) + ((2.0 * HALF - key) == f).astype(f32)
    times = jnp.sum(hit, axis=1, keepdims=True)
    qa = a * (2.0 * math.pi / n)
    qb = b * (2.0 * math.pi / BLK_DEV)
    qc = c * (2.0 * math.pi)
    k2 = qa * qa + qb * qb + qc * qc
    raw = jnp.exp(-k2 / 2000.0) / (k2 + 100.0)
    norm = jnp.sum(times * raw * raw, axis=0, keepdims=True)
    weight = times * raw * lax.rsqrt(norm) * math.sqrt(3.0 / (n * slots))
    weight = weight.reshape(n, grain, 1)
    weight = jnp.concatenate([weight, weight], 1).reshape(rows_all, 1)

    pl.semaphore_wait(barrier, n - 1 + 1 + groups - 1)

    pos_up = remote(p6.at[1], p6.at[0], 0, nxt)
    pos_dn = remote(p6.at[1], p6.at[2], 1, prv)
    feat_up = remote(f6.at[1, 0], f6.at[0, 0], 2, nxt)
    feat_dn = remote(f6.at[1, 0], f6.at[2, 0], 3, prv)
    feat_mate = remote(f6.at[1, 0], f6.at[1, 1], 4, mate)
    fwd_lo = remote(f6.at[0, 0], f6.at[0, 1], 5, mate)
    fwd_hi = remote(f6.at[2, 0], f6.at[2, 1], 6, mate)
    filt_mate = remote(filt_in, fx, 7, mate)
    cot_mate = remote(cm.at[1 - p], c2.at[p], 8, mate)
    for c in (pos_up, pos_dn, feat_up, feat_dn, feat_mate, filt_mate, cot_mate):
        c.start()
    c2[p] = cm[p]

    chunk = 16
    layer_x = s.astype(f32)
    xs = (pos[0:1, :] + layer_x) * (1.0 / n)
    ys = pos[1:2, :] * (1.0 / BLK_DEV)
    zs = pos[2:3, :]

    def reduce_copy(k):
        return pltpu.make_async_remote_copy(
            src_ref=ss.at[lax.rem(s + k, n)], dst_ref=rb.at[s], send_sem=red_s.at[k],
            recv_sem=red_r.at[k], device_id=(lax.rem(s + k, n), q), device_id_type=MESH)

    vs[...] = jnp.concatenate(halves(jnp.concatenate([fm, cmask], 0).T), 1)

    def send_piece(k, carry):
        to = lax.rem(s + k, n)
        for at in range(0, grain, chunk):
            _, a, b, c = lattice((to * grain + at).astype(f32), chunk)
            cosv, sinv = turn_cos_sin(a * xs + b * ys + c * zs)
            th[to, at:at + chunk, :], tl[to, at:at + chunk, :] = halves(cosv)
            th[to, grain + at:grain + at + chunk, :], tl[to, grain + at:grain + at + chunk, :] = halves(sinv)
        two = dot(th[to], vs[...])
        ss[to] = two[:, :pair] + two[:, pair:] + dot(tl[to], vs[:, :pair])

        @pl.when(k < n)
        def _():
            reduce_copy(k).start()

        return carry

    lax.fori_loop(1, n + 1, send_piece, 0)

    pos_up.wait_recv()
    pos_dn.wait_recv()
    pt[...] = p6[1, p].T
    loads[3].wait()
    step = 16
    part_i = cap // PARTS
    chosen = [nbr[p, e] for e in range(NB)]

    for half in range(PARTS):
        def radial(i, carry):
            at = pl.multiple_of(i * step, step)
            own = pt[pl.ds(half * part_i + at, step), :]
            for e in range(NB):
                w = chosen[e]
                far = p6[lax.div(w, BLK_DEV), lax.rem(w, BLK_DEV)]
                offset = (lax.div(w, BLK_DEV) - 1).astype(f32)
                dx = own[:, 0:1] - (far[0:1, :] + offset)
                dy = own[:, 1:2] - far[1:2, :]
                dz = own[:, 2:3] - far[2:3, :]
                sq = jnp.minimum(dx * dx + dy * dy + dz * dz, 1.0)
                left = 1.0 - sq
                u = NRAD * jnp.sqrt(sq) - 0.5
                t = jnp.exp(u)
                g = jnp.exp(-0.5 * u * u) * (0.3 * left * left)
                for r in range(NRAD):
                    if r:
                        g = g * t
                    a, b = halves(g)
                    gh[half, pl.ds(r * part_i + at, step), e * cap:(e + 1) * cap] = a
                    gl[half, pl.ds(r * part_i + at, step), e * cap:(e + 1) * cap] = b
            return carry

        lax.fori_loop(0, part_i // step, radial, 0)
        if half == 0:
            feat_up.wait_recv()
            fwd_lo.start()
            feat_dn.wait_recv()
            fwd_hi.start()

    filt_mate.wait_recv()
    split_filters(fx, 1)

    feat_mate.wait_recv()
    fwd_lo.wait_recv()
    fwd_hi.wait_recv()
    for layer in range(3):
        both = jnp.concatenate([f6[layer, 0], f6[layer, 1]], 0)
        for b in range(BLK_DEV):
            a, c = halves(both[:, b * cap:(b + 1) * cap].T)
            mt[layer * BLK_DEV + b] = jnp.concatenate([a, c], 1)
    for e in range(NB):
        mts[e * cap:(e + 1) * cap, :] = mt[chosen[e]]
    def gather_copy(k):
        return pltpu.make_async_remote_copy(
            src_ref=sg.at[s], dst_ref=sg.at[s], send_sem=gat_s.at[k],
            recv_sem=gat_r.at[k], device_id=(lax.rem(s + k, n), q), device_id_type=MESH)

    def all_gather_start():
        def wait_reduce(k, carry):
            reduce_copy(k).wait_recv()
            return carry

        lax.fori_loop(1, n, wait_reduce, 0)
        rb[s] = ss[s]

        def add_up(k, acc):
            return acc + rb[k]

        sg[s] = lax.fori_loop(0, n, add_up, jnp.zeros((piece, pair), f32))

        def start_gather(k, carry):
            gather_copy(k).start()
            return carry

        lax.fori_loop(1, n, start_gather, 0)

    pre_copies = []
    for half in range(PARTS):
        two = dot(gh[half], mts[...])
        sums = two[:, :pair] + two[:, pair:] + dot(gl[half], mts[:, :pair])
        a, b = halves(sums)
        total = None
        for r in range(NRAD):
            here = slice(r * part_i, (r + 1) * part_i)
            wh, wl = fh[r * pair:(r + 1) * pair, :], fl[r * pair:(r + 1) * pair, :]
            term = dot(jnp.concatenate([a[here], b[here]], 1), jnp.concatenate([wh, wh], 0)) + dot(a[here], wl)
            total = term if r == 0 else total + term
        for k in range(groups):
            ps[half, k] = total[:, k * pair:(k + 1) * pair]
        copies = []
        for k in range(1, groups):
            c = remote(ps.at[half, lax.rem(h + k, groups)], rx.at[half, k - 1], 16 + half * groups + k,
                       (s, lax.rem(q + 2 * k, chans)))
            c.start()
            copies.append(c)
        pre_copies.append(copies)

    all_gather_start()

    cot_mate.wait_recv()
    up_copies = []
    for half in range(PARTS):
        here = slice(half * part_i, (half + 1) * part_i)
        for c in pre_copies[half]:
            c.wait_recv()
        acc = ps[half, h]
        for k in range(1, groups):
            acc = acc + rx[half, k - 1]
        pre = acc.T
        sigma = 1.0 / (1.0 + jnp.exp(-pre))
        act = pre * sigma
        ug[half, h] = jnp.concatenate([c2[0, :, here], c2[1, :, here]], 0) * sigma * (1.0 + pre * (1.0 - sigma))
        copies = []
        for k in range(1, groups):
            c = pltpu.make_async_remote_copy(
                src_ref=ug.at[half, h], dst_ref=ug.at[half, h], send_sem=misc_s.at[16 + (PARTS + half) * groups + k],
                recv_sem=misc_r.at[16 + (PARTS + half) * groups + k],
                device_id=(s, lax.rem(q + 2 * k, chans)), device_id_type=MESH)
            c.start()
            copies.append(c)
        up_copies.append(copies)
        so[0, :, here] = act[:panel]
        so[1, :, here] = act[panel:]
    act_mate = remote(so.at[1 - p], sr, 9, mate)
    act_mate.start()

    pair_cots = []
    for half in range(PARTS):
        for c in up_copies[half]:
            c.wait_recv()
        uh, ul = halves(ug[half].reshape(groups * pair, part_i))
        two = dot(fh[...], jnp.concatenate([uh, ul], 1))
        a, b = halves(two[:, :part_i] + two[:, part_i:] + dot(fl[...], uh))
        a = jnp.concatenate([a[r * pair:(r + 1) * pair] for r in range(NRAD)], 1)
        b = jnp.concatenate([b[r * pair:(r + 1) * pair] for r in range(NRAD)], 1)
        both = jnp.concatenate([a, b], 0)
        pair_cots.append((a, both))
        out = dot(both, gh[half, :, cap:])
        out = out[:pair] + out[pair:] + dot(a, gl[half, :, cap:])
        if half == 0:
            re[:, cap:] = out
        else:
            re[:, cap:] += out
    ret_mates = {}

    def window_sums(layer, entries):
        for blk in range(BLK_DEV):
            w = layer * BLK_DEV + blk
            acc = None
            for e in entries:
                term = jnp.where(chosen[e] == w, re[:, e * cap:(e + 1) * cap], 0.0)
                acc = term if acc is None else acc + term
            wo[layer, blk] = acc[:panel]
            wp[layer, blk] = acc[panel:]
        ret_mates[layer] = remote(wp.at[layer], rw.at[layer], 10 + layer, mate)
        ret_mates[layer].start()

    window_sums(0, range(1, NB))
    window_sums(2, range(1, NB))
    out = None
    for half in range(PARTS):
        a, both = pair_cots[half]
        term = dot(both, gh[half, :, :cap])
        term = term[:pair] + term[pair:] + dot(a, gl[half, :, :cap])
        out = term if half == 0 else out + term
    re[:, :cap] = out
    ret_up = remote(rt.at[1], hb.at[0], 13, nxt)
    ret_dn = remote(rt.at[0], hb.at[1], 14, prv)
    ret_mates[0].wait_recv()
    rt[0] = wo[0] + rw[0]
    ret_dn.start()
    ret_mates[2].wait_recv()
    rt[1] = wo[2] + rw[2]
    ret_up.start()
    window_sums(1, range(NB))

    def wait_gather(k, carry):
        gather_copy(k).wait_recv()
        return carry

    lax.fori_loop(1, n, wait_gather, 0)
    sh, sl = halves((sg[...].reshape(rows_all, pair) * weight).T)
    two = dot(jnp.concatenate([sh, sl], 0), th[...].reshape(rows_all, slots))
    far_part = two[:pair] + two[pair:] + dot(sh, tl[...].reshape(rows_all, slots))
    act_mate.wait_recv()
    mine, other = so[p], sr[...]
    first = jnp.where(p == 0, mine, other)
    second = jnp.where(p == 0, other, mine)
    live_out[...] = jnp.broadcast_to(live, live_out.shape)
    upd[...] = (fm + jnp.concatenate([first, second], 1) + far_part[:panel])
    ret_mates[1].wait_recv()
    part = cmask + far_part[panel:] + jnp.concatenate([wo[1, b] + rw[1, b] for b in range(BLK_DEV)], 1)
    ret_up.wait_recv()
    ret_dn.wait_recv()
    grad[...] = (part + jnp.concatenate([hb[0, b] + hb[1, b] for b in range(BLK_DEV)], 1))

    for c in (pos_up, pos_dn, feat_up, feat_dn, feat_mate, fwd_lo, fwd_hi, filt_mate, cot_mate,
              act_mate, *ret_mates.values(), ret_up, ret_dn, *sum(pre_copies, []), *sum(up_copies, [])):
        c.wait_send()

    def drain(k, carry):
        reduce_copy(k).wait_send()
        gather_copy(k).wait_send()
        return carry

    lax.fori_loop(1, n, drain, 0)


def shards(n, chans, features, positions, counts, neighbours, wavevectors, filters, cotangent):
    panel, slots = features.shape
    cap = slots // BLK_DEV
    pair = 2 * panel
    groups = chans // 2
    piece = -(-(-(-2 * HALF // n)) // 32) * 32
    part_i = cap // PARTS
    vm = pltpu.VMEM
    sm = pltpu.SMEM
    scratch = [
        vm(features.shape, f32),
        vm(positions.shape, f32),
        sm(counts.shape, jnp.int32),
        sm(neighbours.shape, jnp.int32),
        vm(wavevectors.shape, jnp.int32),
        vm(filters.shape, f32),
        vm(cotangent.shape, f32),
        vm((3, 2, panel, slots), f32),
        vm((3, BLK_DEV, 8, cap), f32),
        vm((cap, 8), f32),
        vm(filters.shape, f32),
        vm((NRAD * pair, groups * pair), bf16),
        vm((NRAD * pair, groups * pair), bf16),
        vm((BLK_DEV, panel, cap), f32),
        vm((2, panel, cap), f32),
        vm((PARTS, NRAD * part_i, NB * cap), bf16),
        vm((PARTS, NRAD * part_i, NB * cap), bf16),
        vm((NB * cap, 2 * pair), bf16),
        vm((3 * BLK_DEV, cap, 2 * pair), bf16),
        vm((slots, 2 * pair), bf16),
        vm((n, piece, slots), bf16),
        vm((n, piece, slots), bf16),
        vm((n, piece, pair), f32),
        vm((n, piece, pair), f32),
        vm((n, piece, pair), f32),
        vm((PARTS, groups, part_i, pair), f32),
        vm((PARTS, max(groups - 1, 1), part_i, pair), f32),
        vm((PARTS, groups, pair, part_i), f32),
        vm((2, panel, cap), f32),
        vm((panel, cap), f32),
        vm((pair, NB * cap), f32),
        vm((3, BLK_DEV, panel, cap), f32),
        vm((3, BLK_DEV, panel, cap), f32),
        vm((3, BLK_DEV, panel, cap), f32),
        vm((2, BLK_DEV, panel, cap), f32),
        vm((2, BLK_DEV, panel, cap), f32),
        pltpu.SemaphoreType.DMA((7,)),
        pltpu.SemaphoreType.DMA((16 + 2 * PARTS * groups,)),
        pltpu.SemaphoreType.DMA((16 + 2 * PARTS * groups,)),
        pltpu.SemaphoreType.DMA((n,)),
        pltpu.SemaphoreType.DMA((n,)),
        pltpu.SemaphoreType.DMA((n,)),
        pltpu.SemaphoreType.DMA((n,)),
    ]
    whole = pl.BlockSpec(memory_space=pltpu.VMEM)
    anywhere = pl.BlockSpec(memory_space=pl.ANY)
    out = jax.ShapeDtypeStruct((panel, slots), f32)
    upd, grad, live = pl.pallas_call(
        functools.partial(kernel, n, chans),
        out_shape=(out, out, out),
        in_specs=[anywhere] * 7,
        out_specs=(whole, whole, whole),
        scratch_shapes=scratch,
        compiler_params=pltpu.CompilerParams(
            collective_id=0, has_side_effects=True, vmem_limit_bytes=60 * 1024 * 1024),
    )(features, positions, counts, neighbours, wavevectors, filters, cotangent)
    return upd * live, grad * live


def solution(mesh):
    return jax.shard_map(
        functools.partial(shards, mesh.shape["space"], mesh.shape["chan"]),
        mesh=mesh,
        in_specs=(
            P("chan", "space"),
            P(None, "space"),
            P("space"),
            P("space", None),
            P(),
            P(None, "chan", None),
            P("chan", "space"),
        ),
        out_specs=(P("chan", "space"), P("chan", "space")),
        check_vma=False,
    )
```

```python
import functools
import math

import jax
import jax.numpy as jnp
from jax import lax
from jax.experimental import pallas as pl
from jax.experimental.pallas import tpu as pltpu
from jax.sharding import PartitionSpec as P

NRAD = 8
NB = 4
BLK_DEV = 2
PARTS = 2
MOST = 4
SIDE = 2 * MOST + 1
HALF = (SIDE**3 - 1) // 2
MESH = pl.DeviceIdType.MESH
f32 = jnp.float32
bf16 = jnp.bfloat16


def halves(x):
    high = x.astype(bf16)
    return high, (x - high.astype(f32)).astype(bf16)


def dot(a, b):
    return jnp.dot(a, b, preferred_element_type=f32)


def turn_cos_sin(p):
    r = (p - jnp.floor(p + 0.5)) * math.pi
    s2 = r * r
    s = 1.0 / 6227020800.0
    for n in (-1.0 / 39916800.0, 1.0 / 362880.0, -1.0 / 5040.0, 1.0 / 120.0, -1.0 / 6.0, 1.0):
        s = s * s2 + n
    s = s * r
    c = 1.0 / 479001600.0
    for n in (-1.0 / 3628800.0, 1.0 / 40320.0, -1.0 / 720.0, 1.0 / 24.0, -0.5, 1.0):
        c = c * s2 + n
    return 1.0 - 2.0 * s * s, 2.0 * s * c


def lattice(first, rows):
    f = lax.broadcasted_iota(jnp.int32, (rows, 1), 0).astype(f32) + (first + HALF + 1.0)
    a = jnp.floor((f + 0.5) * (1.0 / (SIDE * SIDE)))
    rest = f - a * (SIDE * SIDE)
    b = jnp.floor((rest + 0.5) * (1.0 / SIDE))
    c = rest - b * SIDE
    return f, a - MOST, b - MOST, c - MOST


def kernel(n, chans, feat_in, pos_in, counts_in, nbr_in, wv_in, filt_in, cot_in, upd, grad, live_out,
           feat, pos, counts, nbr, wv, filt, cot,
           f6, p6, pt, fx, fh, fl, cm, c2, gh, gl, mts, mt, vs, th, tl, ss, rb, sg, ps, rx, ug, so, sr,
           re, wo, wp, rw, rt, hb, load_s, misc_s, misc_r, red_s, red_r, gat_s, gat_r):
    loads = [
        pltpu.make_async_copy(a, b, load_s.at[i])
        for i, (a, b) in enumerate(zip(
            (feat_in, pos_in, counts_in, nbr_in, wv_in, filt_in, cot_in),
            (feat, pos, counts, nbr, wv, filt, cot)))
    ]
    for c in loads:
        c.start()
    panel, slots = feat.shape
    cap = slots // BLK_DEV
    piece = ss.shape[1]
    grain = piece // 2
    rows_all = n * piece
    pair = 2 * panel
    groups = chans // 2
    s = lax.axis_index("space")
    q = lax.axis_index("chan")
    p = lax.rem(q, 2)
    h = lax.div(q, 2)
    mate = (s, q + 1 - 2 * p)
    nxt = (lax.rem(s + 1, n), q)
    prv = (lax.rem(s + n - 1, n), q)

    def remote(src, dst, at, dev):
        return pltpu.make_async_remote_copy(
            src_ref=src, dst_ref=dst, send_sem=misc_s.at[at], recv_sem=misc_r.at[at],
            device_id=dev, device_id_type=MESH)

    barrier = pltpu.get_barrier_semaphore()

    def greet(k, carry):
        pl.semaphore_signal(barrier, inc=1, device_id=(lax.rem(s + k, n), q), device_id_type=MESH)
        return carry

    lax.fori_loop(1, n, greet, 0)
    pl.semaphore_signal(barrier, inc=1, device_id=mate, device_id_type=MESH)
    for k in range(1, groups):
        pl.semaphore_signal(barrier, inc=1, device_id=(s, lax.rem(q + 2 * k, chans)), device_id_type=MESH)

    for at in (0, 1, 2, 6):
        loads[at].wait()
    lane = lax.broadcasted_iota(jnp.int32, (1, slots), 1)
    bound = jnp.where(lane < cap, counts[0], counts[1] + cap)
    live = (lane < bound).astype(f32)
    fm = feat[...] * live
    cmask = cot[...] * live
    f6[1, 0] = fm
    for b in range(BLK_DEV):
        cm[b] = cmask[:, b * cap:(b + 1) * cap]
    p6[1] = jnp.zeros(p6.shape[1:], f32)
    for b in range(BLK_DEV):
        p6[1, b, 0:3, :] = pos[:, b * cap:(b + 1) * cap]

    def split_filters(src, i):
        for r in range(NRAD):
            a, b = halves(src[r] * math.exp(-0.5 * r * r))
            at = r * pair + i * panel
            fh[at:at + panel, :] = a
            fl[at:at + panel, :] = b

    loads[5].wait()
    split_filters(filt, 0)
    loads[4].wait()
    f, a, b, c = lattice(0.0, n * grain)
    wf = wv[...].astype(f32) + MOST
    key = (wf[0:1] * SIDE + wf[1:2]) * SIDE + wf[2:3]
    hit = (key == f).astype(f32) + ((2.0 * HALF - key) == f).astype(f32)
    times = jnp.sum(hit, axis=1, keepdims=True)
    qa = a * (2.0 * math.pi / n)
    qb = b * (2.0 * math.pi / BLK_DEV)
    qc = c * (2.0 * math.pi)
    k2 = qa * qa + qb * qb + qc * qc
    raw = jnp.exp(-k2 / 2000.0) / (k2 + 100.0)
    norm = jnp.sum(times * raw * raw, axis=0, keepdims=True)
    weight = times * raw * lax.rsqrt(norm) * math.sqrt(3.0 / (n * slots))
    weight = weight.reshape(n, grain, 1)
    weight = jnp.concatenate([weight, weight], 1).reshape(rows_all, 1)

    pl.semaphore_wait(barrier, n - 1 + 1 + groups - 1)

    pos_up = remote(p6.at[1], p6.at[0], 0, nxt)
    pos_dn = remote(p6.at[1], p6.at[2], 1, prv)
    feat_up = remote(f6.at[1, 0], f6.at[0, 0], 2, nxt)
    feat_dn = remote(f6.at[1, 0], f6.at[2, 0], 3, prv)
    feat_mate = remote(f6.at[1, 0], f6.at[1, 1], 4, mate)
    fwd_lo = remote(f6.at[0, 0], f6.at[0, 1], 5, mate)
    fwd_hi = remote(f6.at[2, 0], f6.at[2, 1], 6, mate)
    filt_mate = remote(filt_in, fx, 7, mate)
    cot_mate = remote(cm.at[1 - p], c2.at[p], 8, mate)
    for c in (pos_up, pos_dn, feat_up, feat_dn, feat_mate, filt_mate, cot_mate):
        c.start()
    c2[p] = cm[p]

    chunk = 16
    layer_x = s.astype(f32)
    xs = (pos[0:1, :] + layer_x) * (1.0 / n)
    ys = pos[1:2, :] * (1.0 / BLK_DEV)
    zs = pos[2:3, :]

    def reduce_copy(k):
        return pltpu.make_async_remote_copy(
            src_ref=ss.at[lax.rem(s + k, n)], dst_ref=rb.at[s], send_sem=red_s.at[k],
            recv_sem=red_r.at[k], device_id=(lax.rem(s + k, n), q), device_id_type=MESH)

    vs[...] = jnp.concatenate(halves(jnp.concatenate([fm, cmask], 0).T), 1)

    def piece_sums(to, carry):
        for at in range(0, grain, chunk):
            _, a, b, c = lattice((to * grain + at).astype(f32), chunk)
            cosv, sinv = turn_cos_sin(a * xs + b * ys + c * zs)
            th[to, at:at + chunk, :], tl[to, at:at + chunk, :] = halves(cosv)
            th[to, grain + at:grain + at + chunk, :], tl[to, grain + at:grain + at + chunk, :] = halves(sinv)
        two = dot(th[to], vs[...])
        ss[to] = two[:, :pair] + two[:, pair:] + dot(tl[to], vs[:, :pair])
        return carry

    lax.fori_loop(0, n, piece_sums, 0)

    def start_reduce(k, carry):
        reduce_copy(k).start()
        return carry

    pos_up.wait_recv()
    pos_dn.wait_recv()
    pt[...] = p6[1, p].T
    loads[3].wait()
    step = 16
    part_i = cap // PARTS
    chosen = [nbr[p, e] for e in range(NB)]

    for half in range(PARTS):
        def radial(i, carry):
            at = pl.multiple_of(i * step, step)
            own = pt[pl.ds(half * part_i + at, step), :]
            for e in range(NB):
                w = chosen[e]
                far = p6[lax.div(w, BLK_DEV), lax.rem(w, BLK_DEV)]
                offset = (lax.div(w, BLK_DEV) - 1).astype(f32)
                dx = own[:, 0:1] - (far[0:1, :] + offset)
                dy = own[:, 1:2] - far[1:2, :]
                dz = own[:, 2:3] - far[2:3, :]
                sq = jnp.minimum(dx * dx + dy * dy + dz * dz, 1.0)
                left = 1.0 - sq
                u = NRAD * jnp.sqrt(sq) - 0.5
                t = jnp.exp(u)
                g = jnp.exp(-0.5 * u * u) * (0.3 * left * left)
                for r in range(NRAD):
                    if r:
                        g = g * t
                    a, b = halves(g)
                    gh[half, pl.ds(r * part_i + at, step), e * cap:(e + 1) * cap] = a
                    gl[half, pl.ds(r * part_i + at, step), e * cap:(e + 1) * cap] = b
            return carry

        lax.fori_loop(0, part_i // step, radial, 0)
        if half == 0:
            feat_up.wait_recv()
            fwd_lo.start()
            feat_dn.wait_recv()
            fwd_hi.start()
            lax.fori_loop(1, n, start_reduce, 0)

    filt_mate.wait_recv()
    split_filters(fx, 1)

    feat_mate.wait_recv()
    fwd_lo.wait_recv()
    fwd_hi.wait_recv()
    for layer in range(3):
        both = jnp.concatenate([f6[layer, 0], f6[layer, 1]], 0)
        for b in range(BLK_DEV):
            a, c = halves(both[:, b * cap:(b + 1) * cap].T)
            mt[layer * BLK_DEV + b] = jnp.concatenate([a, c], 1)
    for e in range(NB):
        mts[e * cap:(e + 1) * cap, :] = mt[chosen[e]]
    def gather_copy(k):
        return pltpu.make_async_remote_copy(
            src_ref=sg.at[s], dst_ref=sg.at[s], send_sem=gat_s.at[k],
            recv_sem=gat_r.at[k], device_id=(lax.rem(s + k, n), q), device_id_type=MESH)

    def all_gather_start():
        def wait_reduce(k, carry):
            reduce_copy(k).wait_recv()
            return carry

        lax.fori_loop(1, n, wait_reduce, 0)
        rb[s] = ss[s]

        def add_up(k, acc):
            return acc + rb[k]

        sg[s] = lax.fori_loop(0, n, add_up, jnp.zeros((piece, pair), f32))

        def start_gather(k, carry):
            gather_copy(k).start()
            return carry

        lax.fori_loop(1, n, start_gather, 0)

    pre_copies = []
    for half in range(PARTS):
        two = dot(gh[half], mts[...])
        sums = two[:, :pair] + two[:, pair:] + dot(gl[half], mts[:, :pair])
        a, b = halves(sums)
        a = jnp.concatenate([a[r * part_i:(r + 1) * part_i] for r in range(NRAD)], 1)
        b = jnp.concatenate([b[r * part_i:(r + 1) * part_i] for r in range(NRAD)], 1)
        two = dot(jnp.concatenate([a, b], 0), fh[...])
        total = two[:part_i] + two[part_i:] + dot(a, fl[...])
        for k in range(groups):
            ps[half, k] = total[:, k * pair:(k + 1) * pair]
        copies = []
        for k in range(1, groups):
            c = remote(ps.at[half, lax.rem(h + k, groups)], rx.at[half, k - 1], 16 + half * groups + k,
                       (s, lax.rem(q + 2 * k, chans)))
            c.start()
            copies.append(c)
        pre_copies.append(copies)

    all_gather_start()

    cot_mate.wait_recv()
    up_copies = []
    for half in range(PARTS):
        here = slice(half * part_i, (half + 1) * part_i)
        for c in pre_copies[half]:
            c.wait_recv()
        acc = ps[half, h]
        for k in range(1, groups):
            acc = acc + rx[half, k - 1]
        pre = acc.T
        sigma = 1.0 / (1.0 + jnp.exp(-pre))
        act = pre * sigma
        ug[half, h] = jnp.concatenate([c2[0, :, here], c2[1, :, here]], 0) * sigma * (1.0 + pre * (1.0 - sigma))
        copies = []
        for k in range(1, groups):
            c = pltpu.make_async_remote_copy(
                src_ref=ug.at[half, h], dst_ref=ug.at[half, h], send_sem=misc_s.at[16 + (PARTS + half) * groups + k],
                recv_sem=misc_r.at[16 + (PARTS + half) * groups + k],
                device_id=(s, lax.rem(q + 2 * k, chans)), device_id_type=MESH)
            c.start()
            copies.append(c)
        up_copies.append(copies)
        so[0, :, here] = act[:panel]
        so[1, :, here] = act[panel:]
    act_mate = remote(so.at[1 - p], sr, 9, mate)
    act_mate.start()

    pair_cots = []
    for half in range(PARTS):
        for c in up_copies[half]:
            c.wait_recv()
        uh, ul = halves(ug[half].reshape(groups * pair, part_i))
        two = dot(fh[...], jnp.concatenate([uh, ul], 1))
        a, b = halves(two[:, :part_i] + two[:, part_i:] + dot(fl[...], uh))
        a = jnp.concatenate([a[r * pair:(r + 1) * pair] for r in range(NRAD)], 1)
        b = jnp.concatenate([b[r * pair:(r + 1) * pair] for r in range(NRAD)], 1)
        both = jnp.concatenate([a, b], 0)
        pair_cots.append((a, both))
        out = dot(both, gh[half, :, cap:])
        out = out[:pair] + out[pair:] + dot(a, gl[half, :, cap:])
        if half == 0:
            re[:, cap:] = out
        else:
            re[:, cap:] += out
    ret_mates = {}

    def window_sums(layer, entries):
        for blk in range(BLK_DEV):
            w = layer * BLK_DEV + blk
            acc = None
            for e in entries:
                term = jnp.where(chosen[e] == w, re[:, e * cap:(e + 1) * cap], 0.0)
                acc = term if acc is None else acc + term
            wo[layer, blk] = acc[:panel]
            wp[layer, blk] = acc[panel:]
        ret_mates[layer] = remote(wp.at[layer], rw.at[layer], 10 + layer, mate)
        ret_mates[layer].start()

    window_sums(0, range(1, NB))
    window_sums(2, range(1, NB))
    out = None
    for half in range(PARTS):
        a, both = pair_cots[half]
        term = dot(both, gh[half, :, :cap])
        term = term[:pair] + term[pair:] + dot(a, gl[half, :, :cap])
        out = term if half == 0 else out + term
    re[:, :cap] = out
    ret_up = remote(rt.at[1], hb.at[0], 13, nxt)
    ret_dn = remote(rt.at[0], hb.at[1], 14, prv)
    ret_mates[0].wait_recv()
    rt[0] = wo[0] + rw[0]
    ret_dn.start()
    ret_mates[2].wait_recv()
    rt[1] = wo[2] + rw[2]
    ret_up.start()
    window_sums(1, range(NB))

    def wait_gather(k, carry):
        gather_copy(k).wait_recv()
        return carry

    lax.fori_loop(1, n, wait_gather, 0)
    sh, sl = halves((sg[...].reshape(rows_all, pair) * weight).T)
    two = dot(jnp.concatenate([sh, sl], 0), th[...].reshape(rows_all, slots))
    far_part = two[:pair] + two[pair:] + dot(sh, tl[...].reshape(rows_all, slots))
    act_mate.wait_recv()
    mine, other = so[p], sr[...]
    first = jnp.where(p == 0, mine, other)
    second = jnp.where(p == 0, other, mine)
    live_out[...] = jnp.broadcast_to(live, live_out.shape)
    upd[...] = (fm + jnp.concatenate([first, second], 1) + far_part[:panel])
    ret_mates[1].wait_recv()
    part = cmask + far_part[panel:] + jnp.concatenate([wo[1, b] + rw[1, b] for b in range(BLK_DEV)], 1)
    ret_up.wait_recv()
    ret_dn.wait_recv()
    grad[...] = (part + jnp.concatenate([hb[0, b] + hb[1, b] for b in range(BLK_DEV)], 1))

    for c in (pos_up, pos_dn, feat_up, feat_dn, feat_mate, fwd_lo, fwd_hi, filt_mate, cot_mate,
              act_mate, *ret_mates.values(), ret_up, ret_dn, *sum(pre_copies, []), *sum(up_copies, [])):
        c.wait_send()

    def drain(k, carry):
        reduce_copy(k).wait_send()
        gather_copy(k).wait_send()
        return carry

    lax.fori_loop(1, n, drain, 0)


def shards(n, chans, features, positions, counts, neighbours, wavevectors, filters, cotangent):
    panel, slots = features.shape
    cap = slots // BLK_DEV
    pair = 2 * panel
    groups = chans // 2
    piece = -(-(-(-2 * HALF // n)) // 32) * 32
    part_i = cap // PARTS
    vm = pltpu.VMEM
    sm = pltpu.SMEM
    scratch = [
        vm(features.shape, f32),
        vm(positions.shape, f32),
        sm(counts.shape, jnp.int32),
        sm(neighbours.shape, jnp.int32),
        vm(wavevectors.shape, jnp.int32),
        vm(filters.shape, f32),
        vm(cotangent.shape, f32),
        vm((3, 2, panel, slots), f32),
        vm((3, BLK_DEV, 8, cap), f32),
        vm((cap, 8), f32),
        vm(filters.shape, f32),
        vm((NRAD * pair, groups * pair), bf16),
        vm((NRAD * pair, groups * pair), bf16),
        vm((BLK_DEV, panel, cap), f32),
        vm((2, panel, cap), f32),
        vm((PARTS, NRAD * part_i, NB * cap), bf16),
        vm((PARTS, NRAD * part_i, NB * cap), bf16),
        vm((NB * cap, 2 * pair), bf16),
        vm((3 * BLK_DEV, cap, 2 * pair), bf16),
        vm((slots, 2 * pair), bf16),
        vm((n, piece, slots), bf16),
        vm((n, piece, slots), bf16),
        vm((n, piece, pair), f32),
        vm((n, piece, pair), f32),
        vm((n, piece, pair), f32),
        vm((PARTS, groups, part_i, pair), f32),
        vm((PARTS, max(groups - 1, 1), part_i, pair), f32),
        vm((PARTS, groups, pair, part_i), f32),
        vm((2, panel, cap), f32),
        vm((panel, cap), f32),
        vm((pair, NB * cap), f32),
        vm((3, BLK_DEV, panel, cap), f32),
        vm((3, BLK_DEV, panel, cap), f32),
        vm((3, BLK_DEV, panel, cap), f32),
        vm((2, BLK_DEV, panel, cap), f32),
        vm((2, BLK_DEV, panel, cap), f32),
        pltpu.SemaphoreType.DMA((7,)),
        pltpu.SemaphoreType.DMA((16 + 2 * PARTS * groups,)),
        pltpu.SemaphoreType.DMA((16 + 2 * PARTS * groups,)),
        pltpu.SemaphoreType.DMA((n,)),
        pltpu.SemaphoreType.DMA((n,)),
        pltpu.SemaphoreType.DMA((n,)),
        pltpu.SemaphoreType.DMA((n,)),
    ]
    whole = pl.BlockSpec(memory_space=pltpu.VMEM)
    anywhere = pl.BlockSpec(memory_space=pl.ANY)
    out = jax.ShapeDtypeStruct((panel, slots), f32)
    upd, grad, live = pl.pallas_call(
        functools.partial(kernel, n, chans),
        out_shape=(out, out, out),
        in_specs=[anywhere] * 7,
        out_specs=(whole, whole, whole),
        scratch_shapes=scratch,
        compiler_params=pltpu.CompilerParams(
            collective_id=0, has_side_effects=True, vmem_limit_bytes=60 * 1024 * 1024),
    )(features, positions, counts, neighbours, wavevectors, filters, cotangent)
    return upd * live, grad * live


def solution(mesh):
    return jax.shard_map(
        functools.partial(shards, mesh.shape["space"], mesh.shape["chan"]),
        mesh=mesh,
        in_specs=(
            P("chan", "space"),
            P(None, "space"),
            P("space"),
            P("space", None),
            P(),
            P(None, "chan", None),
            P("chan", "space"),
        ),
        out_specs=(P("chan", "space"), P("chan", "space")),
        check_vma=False,
    )
```

```python
import functools
import math

import jax
import jax.numpy as jnp
from jax import lax
from jax.experimental import pallas as pl
from jax.experimental.pallas import tpu as pltpu
from jax.sharding import PartitionSpec as P

NRAD = 8
NB = 4
BLK_DEV = 2
PARTS = 2
LOG2E = math.log2(math.e)
MOST = 4
SIDE = 2 * MOST + 1
HALF = (SIDE**3 - 1) // 2
MESH = pl.DeviceIdType.MESH
f32 = jnp.float32
bf16 = jnp.bfloat16


def halves(x):
    high = x.astype(bf16)
    return high, (x - high.astype(f32)).astype(bf16)


def dot(a, b):
    return jnp.dot(a, b, preferred_element_type=f32)


def turn_cos_sin(p):
    r = (p - jnp.floor(p + 0.5)) * math.pi
    s2 = r * r
    s = 1.0 / 6227020800.0
    for n in (-1.0 / 39916800.0, 1.0 / 362880.0, -1.0 / 5040.0, 1.0 / 120.0, -1.0 / 6.0, 1.0):
        s = s * s2 + n
    s = s * r
    c = 1.0 / 479001600.0
    for n in (-1.0 / 3628800.0, 1.0 / 40320.0, -1.0 / 720.0, 1.0 / 24.0, -0.5, 1.0):
        c = c * s2 + n
    return 1.0 - 2.0 * s * s, 2.0 * s * c


def lattice(first, rows):
    f = lax.broadcasted_iota(jnp.int32, (rows, 1), 0).astype(f32) + (first + HALF + 1.0)
    a = jnp.floor((f + 0.5) * (1.0 / (SIDE * SIDE)))
    rest = f - a * (SIDE * SIDE)
    b = jnp.floor((rest + 0.5) * (1.0 / SIDE))
    c = rest - b * SIDE
    return f, a - MOST, b - MOST, c - MOST


def kernel(n, chans, feat_in, pos_in, counts_in, nbr_in, wv_in, filt_in, cot_in, upd, grad,
           feat, pos, counts, nbr, wv, filt, cot,
           f6, p6, pt, fx, fh, fl, cm, c2, gh, gl, mts, mt, vs, th, tl, ss, rb, sg, ps, rx, ug, so, sr,
           re, wo, wp, rw, rt, hb, load_s, misc_s, misc_r, red_s, red_r, gat_s, gat_r):
    loads = [
        pltpu.make_async_copy(a, b, load_s.at[i])
        for i, (a, b) in enumerate(zip(
            (feat_in, pos_in, counts_in, nbr_in, wv_in, filt_in, cot_in),
            (feat, pos, counts, nbr, wv, filt, cot)))
    ]
    for c in loads:
        c.start()
    panel, slots = feat.shape
    cap = slots // BLK_DEV
    piece = ss.shape[1]
    grain = piece // 2
    rows_all = n * piece
    pair = 2 * panel
    groups = chans // 2
    s = lax.axis_index("space")
    q = lax.axis_index("chan")
    p = lax.rem(q, 2)
    h = lax.div(q, 2)
    mate = (s, q + 1 - 2 * p)
    nxt = (lax.rem(s + 1, n), q)
    prv = (lax.rem(s + n - 1, n), q)

    def remote(src, dst, at, dev):
        return pltpu.make_async_remote_copy(
            src_ref=src, dst_ref=dst, send_sem=misc_s.at[at], recv_sem=misc_r.at[at],
            device_id=dev, device_id_type=MESH)

    barrier = pltpu.get_barrier_semaphore()

    def greet(k, carry):
        pl.semaphore_signal(barrier, inc=1, device_id=(lax.rem(s + k, n), q), device_id_type=MESH)
        return carry

    lax.fori_loop(1, n, greet, 0)
    pl.semaphore_signal(barrier, inc=1, device_id=mate, device_id_type=MESH)
    for k in range(1, groups):
        pl.semaphore_signal(barrier, inc=1, device_id=(s, lax.rem(q + 2 * k, chans)), device_id_type=MESH)

    for at in (0, 1, 2, 6):
        loads[at].wait()
    lane = lax.broadcasted_iota(jnp.int32, (1, slots), 1)
    bound = jnp.where(lane < cap, counts[0], counts[1] + cap)
    live = (lane < bound).astype(f32)
    fm = feat[...] * live
    cmask = cot[...] * live
    f6[1, 0] = fm
    for b in range(BLK_DEV):
        cm[b] = cmask[:, b * cap:(b + 1) * cap]
    p6[1] = jnp.zeros(p6.shape[1:], f32)
    for b in range(BLK_DEV):
        p6[1, b, 0:3, :] = pos[:, b * cap:(b + 1) * cap]

    def split_filters(src, i):
        for r in range(NRAD):
            a, b = halves(src[r] * math.exp(-0.5 * r * r))
            at = r * pair + i * panel
            fh[at:at + panel, :] = a
            fl[at:at + panel, :] = b

    loads[5].wait()
    split_filters(filt, 0)
    loads[4].wait()
    f, a, b, c = lattice(0.0, n * grain)
    wf = wv[...].astype(f32) + MOST
    key = (wf[0:1] * SIDE + wf[1:2]) * SIDE + wf[2:3]
    hit = (key == f).astype(f32) + ((2.0 * HALF - key) == f).astype(f32)
    times = jnp.sum(hit, axis=1, keepdims=True)
    qa = a * (2.0 * math.pi / n)
    qb = b * (2.0 * math.pi / BLK_DEV)
    qc = c * (2.0 * math.pi)
    k2 = qa * qa + qb * qb + qc * qc
    raw = jnp.exp(-k2 / 2000.0) / (k2 + 100.0)
    norm = jnp.sum(times * raw * raw, axis=0, keepdims=True)
    weight = times * raw * lax.rsqrt(norm) * math.sqrt(3.0 / (n * slots))
    weight = weight.reshape(n, grain, 1)
    weight = jnp.concatenate([weight, weight], 1).reshape(rows_all, 1)

    pl.semaphore_wait(barrier, n - 1 + 1 + groups - 1)

    pos_up = remote(p6.at[1], p6.at[0], 0, nxt)
    pos_dn = remote(p6.at[1], p6.at[2], 1, prv)
    feat_up = remote(f6.at[1, 0], f6.at[0, 0], 2, nxt)
    feat_dn = remote(f6.at[1, 0], f6.at[2, 0], 3, prv)
    feat_mate = remote(f6.at[1, 0], f6.at[1, 1], 4, mate)
    fwd_lo = remote(f6.at[0, 0], f6.at[0, 1], 5, mate)
    fwd_hi = remote(f6.at[2, 0], f6.at[2, 1], 6, mate)
    filt_mate = remote(filt_in, fx, 7, mate)
    cot_mate = remote(cm.at[1 - p], c2.at[p], 8, mate)
    for c in (pos_up, pos_dn, feat_up, feat_dn, feat_mate, filt_mate, cot_mate):
        c.start()
    c2[p] = cm[p]

    chunk = 16
    layer_x = s.astype(f32)
    xs = (pos[0:1, :] + layer_x) * (1.0 / n)
    ys = pos[1:2, :] * (1.0 / BLK_DEV)
    zs = pos[2:3, :]

    def reduce_copy(k):
        return pltpu.make_async_remote_copy(
            src_ref=ss.at[lax.rem(s + k, n)], dst_ref=rb.at[s], send_sem=red_s.at[k],
            recv_sem=red_r.at[k], device_id=(lax.rem(s + k, n), q), device_id_type=MESH)

    vs[...] = jnp.concatenate(halves(jnp.concatenate([fm, cmask], 0).T), 1)

    def piece_sums(to, carry):
        for at in range(0, grain, chunk):
            _, a, b, c = lattice((to * grain + at).astype(f32), chunk)
            cosv, sinv = turn_cos_sin(a * xs + b * ys + c * zs)
            th[to, at:at + chunk, :], tl[to, at:at + chunk, :] = halves(cosv)
            th[to, grain + at:grain + at + chunk, :], tl[to, grain + at:grain + at + chunk, :] = halves(sinv)
        two = dot(th[to], vs[...])
        ss[to] = two[:, :pair] + two[:, pair:] + dot(tl[to], vs[:, :pair])
        return carry

    lax.fori_loop(0, n, piece_sums, 0)

    def start_reduce(k, carry):
        reduce_copy(k).start()
        return carry

    pos_up.wait_recv()
    pos_dn.wait_recv()
    pt[...] = p6[1, p].T
    loads[3].wait()
    step = 16
    part_i = cap // PARTS
    chosen = [nbr[p, e] for e in range(NB)]

    for half in range(PARTS):
        def radial(i, carry):
            at = pl.multiple_of(i * step, step)
            own = pt[pl.ds(half * part_i + at, step), :]
            for e in range(NB):
                w = chosen[e]
                far = p6[lax.div(w, BLK_DEV), lax.rem(w, BLK_DEV)]
                offset = (lax.div(w, BLK_DEV) - 1).astype(f32)
                dx = own[:, 0:1] - (far[0:1, :] + offset)
                dy = own[:, 1:2] - far[1:2, :]
                dz = own[:, 2:3] - far[2:3, :]
                sq = jnp.minimum(dx * dx + dy * dy + dz * dz, 1.0)
                left = 1.0 - sq
                u = (sq * NRAD) * lax.rsqrt(jnp.maximum(sq, 1e-30)) - 0.5
                t = jnp.exp2(u * LOG2E)
                g = jnp.exp2((u * u) * (-0.5 * LOG2E)) * (0.3 * left * left)
                for r in range(NRAD):
                    if r:
                        g = g * t
                    a, b = halves(g)
                    gh[half, pl.ds(r * part_i + at, step), e * cap:(e + 1) * cap] = a
                    gl[half, pl.ds(r * part_i + at, step), e * cap:(e + 1) * cap] = b
            return carry

        lax.fori_loop(0, part_i // step, radial, 0)
        if half == 0:
            feat_up.wait_recv()
            fwd_lo.start()
            feat_dn.wait_recv()
            fwd_hi.start()
            lax.fori_loop(1, n, start_reduce, 0)

    filt_mate.wait_recv()
    split_filters(fx, 1)

    feat_mate.wait_recv()
    fwd_lo.wait_recv()
    fwd_hi.wait_recv()
    for layer in range(3):
        both = jnp.concatenate([f6[layer, 0], f6[layer, 1]], 0)
        for b in range(BLK_DEV):
            a, c = halves(both[:, b * cap:(b + 1) * cap].T)
            mt[layer * BLK_DEV + b] = jnp.concatenate([a, c], 1)
    for e in range(NB):
        mts[e * cap:(e + 1) * cap, :] = mt[chosen[e]]
    def gather_copy(k):
        return pltpu.make_async_remote_copy(
            src_ref=sg.at[s], dst_ref=sg.at[s], send_sem=gat_s.at[k],
            recv_sem=gat_r.at[k], device_id=(lax.rem(s + k, n), q), device_id_type=MESH)

    def all_gather_start():
        def wait_reduce(k, carry):
            reduce_copy(k).wait_recv()
            return carry

        lax.fori_loop(1, n, wait_reduce, 0)
        rb[s] = ss[s]

        def add_up(k, acc):
            return acc + rb[k]

        sg[s] = lax.fori_loop(0, n, add_up, jnp.zeros((piece, pair), f32))

        def start_gather(k, carry):
            gather_copy(k).start()
            return carry

        lax.fori_loop(1, n, start_gather, 0)

    pre_copies = []
    for half in range(PARTS):
        two = dot(gh[half], mts[...])
        sums = two[:, :pair] + two[:, pair:] + dot(gl[half], mts[:, :pair])
        a, b = halves(sums)
        a = jnp.concatenate([a[r * part_i:(r + 1) * part_i] for r in range(NRAD)], 1)
        b = jnp.concatenate([b[r * part_i:(r + 1) * part_i] for r in range(NRAD)], 1)
        two = dot(jnp.concatenate([a, b], 0), fh[...])
        total = two[:part_i] + two[part_i:] + dot(a, fl[...])
        for k in range(groups):
            ps[half, k] = total[:, k * pair:(k + 1) * pair]
        copies = []
        for k in range(1, groups):
            c = remote(ps.at[half, lax.rem(h + k, groups)], rx.at[half, k - 1], 16 + half * groups + k,
                       (s, lax.rem(q + 2 * k, chans)))
            c.start()
            copies.append(c)
        pre_copies.append(copies)

    all_gather_start()

    cot_mate.wait_recv()
    up_copies = []
    for half in range(PARTS):
        here = slice(half * part_i, (half + 1) * part_i)
        for c in pre_copies[half]:
            c.wait_recv()
        acc = ps[half, h]
        for k in range(1, groups):
            acc = acc + rx[half, k - 1]
        pre = acc.T
        sigma = 1.0 / (1.0 + jnp.exp(-pre))
        act = pre * sigma
        ug[half, h] = jnp.concatenate([c2[0, :, here], c2[1, :, here]], 0) * sigma * (1.0 + pre * (1.0 - sigma))
        copies = []
        for k in range(1, groups):
            c = pltpu.make_async_remote_copy(
                src_ref=ug.at[half, h], dst_ref=ug.at[half, h], send_sem=misc_s.at[16 + (PARTS + half) * groups + k],
                recv_sem=misc_r.at[16 + (PARTS + half) * groups + k],
                device_id=(s, lax.rem(q + 2 * k, chans)), device_id_type=MESH)
            c.start()
            copies.append(c)
        up_copies.append(copies)
        so[0, :, here] = act[:panel]
        so[1, :, here] = act[panel:]
    act_mate = remote(so.at[1 - p], sr, 9, mate)
    act_mate.start()

    pair_cots = []
    for half in range(PARTS):
        for c in up_copies[half]:
            c.wait_recv()
        uh, ul = halves(ug[half].reshape(groups * pair, part_i))
        two = dot(fh[...], jnp.concatenate([uh, ul], 1))
        a, b = halves(two[:, :part_i] + two[:, part_i:] + dot(fl[...], uh))
        a = jnp.concatenate([a[r * pair:(r + 1) * pair] for r in range(NRAD)], 1)
        b = jnp.concatenate([b[r * pair:(r + 1) * pair] for r in range(NRAD)], 1)
        both = jnp.concatenate([a, b], 0)
        pair_cots.append((a, both))
        out = dot(both, gh[half, :, cap:])
        out = out[:pair] + out[pair:] + dot(a, gl[half, :, cap:])
        if half == 0:
            re[:, cap:] = out
        else:
            re[:, cap:] += out
    ret_mates = {}

    def window_sums(layer, entries):
        for blk in range(BLK_DEV):
            w = layer * BLK_DEV + blk
            acc = None
            for e in entries:
                term = jnp.where(chosen[e] == w, re[:, e * cap:(e + 1) * cap], 0.0)
                acc = term if acc is None else acc + term
            wo[layer, blk] = acc[:panel]
            wp[layer, blk] = acc[panel:]
        ret_mates[layer] = remote(wp.at[layer], rw.at[layer], 10 + layer, mate)
        ret_mates[layer].start()

    window_sums(0, range(1, NB))
    window_sums(2, range(1, NB))
    out = None
    for half in range(PARTS):
        a, both = pair_cots[half]
        term = dot(both, gh[half, :, :cap])
        term = term[:pair] + term[pair:] + dot(a, gl[half, :, :cap])
        out = term if half == 0 else out + term
    re[:, :cap] = out
    ret_up = remote(rt.at[1], hb.at[0], 13, nxt)
    ret_dn = remote(rt.at[0], hb.at[1], 14, prv)
    ret_mates[0].wait_recv()
    rt[0] = wo[0] + rw[0]
    ret_dn.start()
    ret_mates[2].wait_recv()
    rt[1] = wo[2] + rw[2]
    ret_up.start()
    window_sums(1, range(NB))

    def wait_gather(k, carry):
        gather_copy(k).wait_recv()
        return carry

    lax.fori_loop(1, n, wait_gather, 0)
    sh, sl = halves((sg[...].reshape(rows_all, pair) * weight).T)
    two = dot(jnp.concatenate([sh, sl], 0), th[...].reshape(rows_all, slots))
    far_part = two[:pair] + two[pair:] + dot(sh, tl[...].reshape(rows_all, slots))
    act_mate.wait_recv()
    mine, other = so[p], sr[...]
    first = jnp.where(p == 0, mine, other)
    second = jnp.where(p == 0, other, mine)
    upd[...] = live * (fm + jnp.concatenate([first, second], 1) + far_part[:panel])
    ret_mates[1].wait_recv()
    part = cmask + far_part[panel:] + jnp.concatenate([wo[1, b] + rw[1, b] for b in range(BLK_DEV)], 1)
    ret_up.wait_recv()
    ret_dn.wait_recv()
    grad[...] = live * (part + jnp.concatenate([hb[0, b] + hb[1, b] for b in range(BLK_DEV)], 1))

    for c in (pos_up, pos_dn, feat_up, feat_dn, feat_mate, fwd_lo, fwd_hi, filt_mate, cot_mate,
              act_mate, *ret_mates.values(), ret_up, ret_dn, *sum(pre_copies, []), *sum(up_copies, [])):
        c.wait_send()

    def drain(k, carry):
        reduce_copy(k).wait_send()
        gather_copy(k).wait_send()
        return carry

    lax.fori_loop(1, n, drain, 0)


def finish(upd_in, grad_in, upd, grad, sem):
    copies = [pltpu.make_async_copy(upd_in, upd, sem.at[0]), pltpu.make_async_copy(grad_in, grad, sem.at[1])]
    for c in copies:
        c.start()
    for c in copies:
        c.wait()


def shards(n, chans, features, positions, counts, neighbours, wavevectors, filters, cotangent):
    panel, slots = features.shape
    cap = slots // BLK_DEV
    pair = 2 * panel
    groups = chans // 2
    piece = -(-(-(-2 * HALF // n)) // 32) * 32
    part_i = cap // PARTS
    vm = pltpu.VMEM
    sm = pltpu.SMEM
    scratch = [
        vm(features.shape, f32),
        vm(positions.shape, f32),
        sm(counts.shape, jnp.int32),
        sm(neighbours.shape, jnp.int32),
        vm(wavevectors.shape, jnp.int32),
        vm(filters.shape, f32),
        vm(cotangent.shape, f32),
        vm((3, 2, panel, slots), f32),
        vm((3, BLK_DEV, 8, cap), f32),
        vm((cap, 8), f32),
        vm(filters.shape, f32),
        vm((NRAD * pair, groups * pair), bf16),
        vm((NRAD * pair, groups * pair), bf16),
        vm((BLK_DEV, panel, cap), f32),
        vm((2, panel, cap), f32),
        vm((PARTS, NRAD * part_i, NB * cap), bf16),
        vm((PARTS, NRAD * part_i, NB * cap), bf16),
        vm((NB * cap, 2 * pair), bf16),
        vm((3 * BLK_DEV, cap, 2 * pair), bf16),
        vm((slots, 2 * pair), bf16),
        vm((n, piece, slots), bf16),
        vm((n, piece, slots), bf16),
        vm((n, piece, pair), f32),
        vm((n, piece, pair), f32),
        vm((n, piece, pair), f32),
        vm((PARTS, groups, part_i, pair), f32),
        vm((PARTS, max(groups - 1, 1), part_i, pair), f32),
        vm((PARTS, groups, pair, part_i), f32),
        vm((2, panel, cap), f32),
        vm((panel, cap), f32),
        vm((pair, NB * cap), f32),
        vm((3, BLK_DEV, panel, cap), f32),
        vm((3, BLK_DEV, panel, cap), f32),
        vm((3, BLK_DEV, panel, cap), f32),
        vm((2, BLK_DEV, panel, cap), f32),
        vm((2, BLK_DEV, panel, cap), f32),
        pltpu.SemaphoreType.DMA((7,)),
        pltpu.SemaphoreType.DMA((16 + 2 * PARTS * groups,)),
        pltpu.SemaphoreType.DMA((16 + 2 * PARTS * groups,)),
        pltpu.SemaphoreType.DMA((n,)),
        pltpu.SemaphoreType.DMA((n,)),
        pltpu.SemaphoreType.DMA((n,)),
        pltpu.SemaphoreType.DMA((n,)),
    ]
    whole = pl.BlockSpec(memory_space=pltpu.VMEM)
    anywhere = pl.BlockSpec(memory_space=pl.ANY)
    out = jax.ShapeDtypeStruct((panel, slots), f32)
    results = pl.pallas_call(
        functools.partial(kernel, n, chans),
        out_shape=(out, out),
        in_specs=[anywhere] * 7,
        out_specs=(whole, whole),
        scratch_shapes=scratch,
        compiler_params=pltpu.CompilerParams(
            collective_id=0, has_side_effects=True, vmem_limit_bytes=60 * 1024 * 1024),
    )(features, positions, counts, neighbours, wavevectors, filters, cotangent)
    return pl.pallas_call(
        finish,
        out_shape=(out, out),
        in_specs=[anywhere] * 2,
        out_specs=(anywhere, anywhere),
        scratch_shapes=[pltpu.SemaphoreType.DMA((2,))],
        compiler_params=pltpu.CompilerParams(vmem_limit_bytes=60 * 1024 * 1024),
    )(*results)


def solution(mesh):
    return jax.shard_map(
        functools.partial(shards, mesh.shape["space"], mesh.shape["chan"]),
        mesh=mesh,
        in_specs=(
            P("chan", "space"),
            P(None, "space"),
            P("space"),
            P("space", None),
            P(),
            P(None, "chan", None),
            P("chan", "space"),
        ),
        out_specs=(P("chan", "space"), P("chan", "space")),
        check_vma=False,
    )
```

```python
import functools
import math

import jax
import jax.numpy as jnp
from jax import lax
from jax.experimental import pallas as pl
from jax.experimental.pallas import tpu as pltpu
from jax.sharding import PartitionSpec as P

NRAD = 8
NB = 4
BLK_DEV = 2
PARTS = 2
LOG2E = math.log2(math.e)
MOST = 4
SIDE = 2 * MOST + 1
HALF = (SIDE**3 - 1) // 2
MESH = pl.DeviceIdType.MESH
f32 = jnp.float32
bf16 = jnp.bfloat16


def halves(x):
    high = x.astype(bf16)
    return high, (x - high.astype(f32)).astype(bf16)


def dot(a, b):
    return jnp.dot(a, b, preferred_element_type=f32)


def turn_cos_sin(p):
    r = (p - jnp.floor(p + 0.5)) * math.pi
    s2 = r * r
    s = 1.0 / 6227020800.0
    for n in (-1.0 / 39916800.0, 1.0 / 362880.0, -1.0 / 5040.0, 1.0 / 120.0, -1.0 / 6.0, 1.0):
        s = s * s2 + n
    s = s * r
    c = 1.0 / 479001600.0
    for n in (-1.0 / 3628800.0, 1.0 / 40320.0, -1.0 / 720.0, 1.0 / 24.0, -0.5, 1.0):
        c = c * s2 + n
    return 1.0 - 2.0 * s * s, 2.0 * s * c


def lattice(first, rows):
    f = lax.broadcasted_iota(jnp.int32, (rows, 1), 0).astype(f32) + (first + HALF + 1.0)
    a = jnp.floor((f + 0.5) * (1.0 / (SIDE * SIDE)))
    rest = f - a * (SIDE * SIDE)
    b = jnp.floor((rest + 0.5) * (1.0 / SIDE))
    c = rest - b * SIDE
    return f, a - MOST, b - MOST, c - MOST


def kernel(n, chans, feat_in, pos_in, counts_in, nbr_in, wv_in, filt_in, cot_in, upd, grad,
           feat, pos, counts, nbr, wv, filt, cot,
           f6, p6, pt, fx, fh, fl, cm, c2, gh, gl, mts, mt, vs, th, tl, ss, rb, sg, ps, rx, ug, so, sr,
           re, wo, wp, rw, rt, hb, load_s, misc_s, misc_r, red_s, red_r, gat_s, gat_r):
    loads = [
        pltpu.make_async_copy(a, b, load_s.at[i])
        for i, (a, b) in enumerate(zip(
            (feat_in, pos_in, counts_in, nbr_in, wv_in, filt_in, cot_in),
            (feat, pos, counts, nbr, wv, filt, cot)))
    ]
    for c in loads:
        c.start()
    panel, slots = feat.shape
    cap = slots // BLK_DEV
    piece = ss.shape[1]
    grain = piece // 2
    rows_all = n * piece
    pair = 2 * panel
    groups = chans // 2
    s = lax.axis_index("space")
    q = lax.axis_index("chan")
    p = lax.rem(q, 2)
    h = lax.div(q, 2)
    mate = (s, q + 1 - 2 * p)
    nxt = (lax.rem(s + 1, n), q)
    prv = (lax.rem(s + n - 1, n), q)

    def remote(src, dst, at, dev):
        return pltpu.make_async_remote_copy(
            src_ref=src, dst_ref=dst, send_sem=misc_s.at[at], recv_sem=misc_r.at[at],
            device_id=dev, device_id_type=MESH)

    barrier = pltpu.get_barrier_semaphore()

    def greet(k, carry):
        pl.semaphore_signal(barrier, inc=1, device_id=(lax.rem(s + k, n), q), device_id_type=MESH)
        return carry

    lax.fori_loop(1, n, greet, 0)
    pl.semaphore_signal(barrier, inc=1, device_id=mate, device_id_type=MESH)
    for k in range(1, groups):
        pl.semaphore_signal(barrier, inc=1, device_id=(s, lax.rem(q + 2 * k, chans)), device_id_type=MESH)

    for at in (0, 1, 2, 6):
        loads[at].wait()
    lane = lax.broadcasted_iota(jnp.int32, (1, slots), 1)
    bound = jnp.where(lane < cap, counts[0], counts[1] + cap)
    live = (lane < bound).astype(f32)
    fm = feat[...] * live
    cmask = cot[...] * live
    f6[1, 0] = fm
    for b in range(BLK_DEV):
        cm[b] = cmask[:, b * cap:(b + 1) * cap]
    p6[1] = jnp.zeros(p6.shape[1:], f32)
    for b in range(BLK_DEV):
        p6[1, b, 0:3, :] = pos[:, b * cap:(b + 1) * cap]

    def split_filters(src, i):
        for r in range(NRAD):
            a, b = halves(src[r] * math.exp(-0.5 * r * r))
            at = r * pair + i * panel
            fh[at:at + panel, :] = a
            fl[at:at + panel, :] = b

    pl.semaphore_wait(barrier, n - 1 + 1 + groups - 1)

    pos_up = remote(p6.at[1], p6.at[0], 0, nxt)
    pos_dn = remote(p6.at[1], p6.at[2], 1, prv)
    feat_up = remote(f6.at[1, 0], f6.at[0, 0], 2, nxt)
    feat_dn = remote(f6.at[1, 0], f6.at[2, 0], 3, prv)
    feat_mate = remote(f6.at[1, 0], f6.at[1, 1], 4, mate)
    fwd_lo = remote(f6.at[0, 0], f6.at[0, 1], 5, mate)
    fwd_hi = remote(f6.at[2, 0], f6.at[2, 1], 6, mate)
    filt_mate = remote(filt_in, fx, 7, mate)
    cot_mate = remote(cm.at[1 - p], c2.at[p], 8, mate)
    for c in (pos_up, pos_dn, feat_up, feat_dn, feat_mate, filt_mate, cot_mate):
        c.start()
    c2[p] = cm[p]

    chunk = 16
    layer_x = s.astype(f32)
    xs = (pos[0:1, :] + layer_x) * (1.0 / n)
    ys = pos[1:2, :] * (1.0 / BLK_DEV)
    zs = pos[2:3, :]

    def reduce_copy(k):
        return pltpu.make_async_remote_copy(
            src_ref=ss.at[lax.rem(s + k, n)], dst_ref=rb.at[s], send_sem=red_s.at[k],
            recv_sem=red_r.at[k], device_id=(lax.rem(s + k, n), q), device_id_type=MESH)

    vs[...] = jnp.concatenate(halves(jnp.concatenate([fm, cmask], 0).T), 1)

    def piece_sums(to, carry):
        for at in range(0, grain, chunk):
            _, a, b, c = lattice((to * grain + at).astype(f32), chunk)
            cosv, sinv = turn_cos_sin(a * xs + b * ys + c * zs)
            th[to, at:at + chunk, :], tl[to, at:at + chunk, :] = halves(cosv)
            th[to, grain + at:grain + at + chunk, :], tl[to, grain + at:grain + at + chunk, :] = halves(sinv)
        two = dot(th[to], vs[...])
        ss[to] = two[:, :pair] + two[:, pair:] + dot(tl[to], vs[:, :pair])
        return carry

    lax.fori_loop(0, n, piece_sums, 0)

    def start_reduce(k, carry):
        reduce_copy(k).start()
        return carry

    pos_up.wait_recv()
    pos_dn.wait_recv()
    pt[...] = p6[1, p].T
    loads[3].wait()
    step = 16
    part_i = cap // PARTS
    chosen = [nbr[p, e] for e in range(NB)]

    for half in range(PARTS):
        def radial(i, carry):
            at = pl.multiple_of(i * step, step)
            own = pt[pl.ds(half * part_i + at, step), :]
            for e in range(NB):
                w = chosen[e]
                far = p6[lax.div(w, BLK_DEV), lax.rem(w, BLK_DEV)]
                offset = (lax.div(w, BLK_DEV) - 1).astype(f32)
                dx = own[:, 0:1] - (far[0:1, :] + offset)
                dy = own[:, 1:2] - far[1:2, :]
                dz = own[:, 2:3] - far[2:3, :]
                sq = jnp.minimum(dx * dx + dy * dy + dz * dz, 1.0)
                left = 1.0 - sq
                u = (sq * NRAD) * lax.rsqrt(jnp.maximum(sq, 1e-30)) - 0.5
                t = jnp.exp2(u * LOG2E)
                g = jnp.exp2((u * u) * (-0.5 * LOG2E)) * (0.3 * left * left)
                for r in range(NRAD):
                    if r:
                        g = g * t
                    a, b = halves(g)
                    gh[half, pl.ds(r * part_i + at, step), e * cap:(e + 1) * cap] = a
                    gl[half, pl.ds(r * part_i + at, step), e * cap:(e + 1) * cap] = b
            return carry

        lax.fori_loop(0, part_i // step, radial, 0)
        if half == 0:
            loads[5].wait()
            split_filters(filt, 0)
            filt_mate.wait_recv()
            split_filters(fx, 1)
            feat_up.wait_recv()
            fwd_lo.start()
            feat_dn.wait_recv()
            fwd_hi.start()
            lax.fori_loop(1, n, start_reduce, 0)

    feat_mate.wait_recv()
    fwd_lo.wait_recv()
    fwd_hi.wait_recv()
    for layer in range(3):
        both = jnp.concatenate([f6[layer, 0], f6[layer, 1]], 0)
        for b in range(BLK_DEV):
            a, c = halves(both[:, b * cap:(b + 1) * cap].T)
            mt[layer * BLK_DEV + b] = jnp.concatenate([a, c], 1)
    for e in range(NB):
        mts[e * cap:(e + 1) * cap, :] = mt[chosen[e]]
    def gather_copy(k):
        return pltpu.make_async_remote_copy(
            src_ref=sg.at[s], dst_ref=sg.at[s], send_sem=gat_s.at[k],
            recv_sem=gat_r.at[k], device_id=(lax.rem(s + k, n), q), device_id_type=MESH)

    def all_gather_start():
        def wait_reduce(k, carry):
            reduce_copy(k).wait_recv()
            return carry

        lax.fori_loop(1, n, wait_reduce, 0)
        rb[s] = ss[s]

        def add_up(k, acc):
            return acc + rb[k]

        sg[s] = lax.fori_loop(0, n, add_up, jnp.zeros((piece, pair), f32))

        def start_gather(k, carry):
            gather_copy(k).start()
            return carry

        lax.fori_loop(1, n, start_gather, 0)

    pre_copies = []
    for half in range(PARTS):
        two = dot(gh[half], mts[...])
        sums = two[:, :pair] + two[:, pair:] + dot(gl[half], mts[:, :pair])
        a, b = halves(sums)
        a = jnp.concatenate([a[r * part_i:(r + 1) * part_i] for r in range(NRAD)], 1)
        b = jnp.concatenate([b[r * part_i:(r + 1) * part_i] for r in range(NRAD)], 1)
        two = dot(jnp.concatenate([a, b], 0), fh[...])
        total = two[:part_i] + two[part_i:] + dot(a, fl[...])
        for k in range(groups):
            ps[half, k] = total[:, k * pair:(k + 1) * pair]
        copies = []
        for k in range(1, groups):
            c = remote(ps.at[half, lax.rem(h + k, groups)], rx.at[half, k - 1], 16 + half * groups + k,
                       (s, lax.rem(q + 2 * k, chans)))
            c.start()
            copies.append(c)
        pre_copies.append(copies)

    all_gather_start()

    cot_mate.wait_recv()
    up_copies = []
    for half in range(PARTS):
        here = slice(half * part_i, (half + 1) * part_i)
        for c in pre_copies[half]:
            c.wait_recv()
        acc = ps[half, h]
        for k in range(1, groups):
            acc = acc + rx[half, k - 1]
        pre = acc.T
        sigma = 1.0 / (1.0 + jnp.exp(-pre))
        act = pre * sigma
        ug[half, h] = jnp.concatenate([c2[0, :, here], c2[1, :, here]], 0) * sigma * (1.0 + pre * (1.0 - sigma))
        copies = []
        for k in range(1, groups):
            c = pltpu.make_async_remote_copy(
                src_ref=ug.at[half, h], dst_ref=ug.at[half, h], send_sem=misc_s.at[16 + (PARTS + half) * groups + k],
                recv_sem=misc_r.at[16 + (PARTS + half) * groups + k],
                device_id=(s, lax.rem(q + 2 * k, chans)), device_id_type=MESH)
            c.start()
            copies.append(c)
        up_copies.append(copies)
        so[0, :, here] = act[:panel]
        so[1, :, here] = act[panel:]
    act_mate = remote(so.at[1 - p], sr, 9, mate)
    act_mate.start()

    loads[4].wait()
    f, a, b, c = lattice(0.0, n * grain)
    wf = wv[...].astype(f32) + MOST
    key = (wf[0:1] * SIDE + wf[1:2]) * SIDE + wf[2:3]
    hit = (key == f).astype(f32) + ((2.0 * HALF - key) == f).astype(f32)
    times = jnp.sum(hit, axis=1, keepdims=True)
    qa = a * (2.0 * math.pi / n)
    qb = b * (2.0 * math.pi / BLK_DEV)
    qc = c * (2.0 * math.pi)
    k2 = qa * qa + qb * qb + qc * qc
    raw = jnp.exp(-k2 / 2000.0) / (k2 + 100.0)
    norm = jnp.sum(times * raw * raw, axis=0, keepdims=True)
    weight = times * raw * lax.rsqrt(norm) * math.sqrt(3.0 / (n * slots))
    weight = weight.reshape(n, grain, 1)
    weight = jnp.concatenate([weight, weight], 1).reshape(rows_all, 1)

    pair_cots = []
    for half in range(PARTS):
        for c in up_copies[half]:
            c.wait_recv()
        uh, ul = halves(ug[half].reshape(groups * pair, part_i))
        two = dot(fh[...], jnp.concatenate([uh, ul], 1))
        a, b = halves(two[:, :part_i] + two[:, part_i:] + dot(fl[...], uh))
        a = jnp.concatenate([a[r * pair:(r + 1) * pair] for r in range(NRAD)], 1)
        b = jnp.concatenate([b[r * pair:(r + 1) * pair] for r in range(NRAD)], 1)
        both = jnp.concatenate([a, b], 0)
        pair_cots.append((a, both))
        out = dot(both, gh[half, :, cap:])
        out = out[:pair] + out[pair:] + dot(a, gl[half, :, cap:])
        if half == 0:
            re[:, cap:] = out
        else:
            re[:, cap:] += out
    ret_mates = {}

    def window_sums(layer, entries):
        for blk in range(BLK_DEV):
            w = layer * BLK_DEV + blk
            acc = None
            for e in entries:
                term = jnp.where(chosen[e] == w, re[:, e * cap:(e + 1) * cap], 0.0)
                acc = term if acc is None else acc + term
            wo[layer, blk] = acc[:panel]
            wp[layer, blk] = acc[panel:]
        ret_mates[layer] = remote(wp.at[layer], rw.at[layer], 10 + layer, mate)
        ret_mates[layer].start()

    window_sums(0, range(1, NB))
    window_sums(2, range(1, NB))
    out = None
    for half in range(PARTS):
        a, both = pair_cots[half]
        term = dot(both, gh[half, :, :cap])
        term = term[:pair] + term[pair:] + dot(a, gl[half, :, :cap])
        out = term if half == 0 else out + term
    re[:, :cap] = out
    ret_up = remote(rt.at[1], hb.at[0], 13, nxt)
    ret_dn = remote(rt.at[0], hb.at[1], 14, prv)
    ret_mates[0].wait_recv()
    rt[0] = wo[0] + rw[0]
    ret_dn.start()
    ret_mates[2].wait_recv()
    rt[1] = wo[2] + rw[2]
    ret_up.start()
    window_sums(1, range(NB))

    def wait_gather(k, carry):
        gather_copy(k).wait_recv()
        return carry

    lax.fori_loop(1, n, wait_gather, 0)
    sh, sl = halves((sg[...].reshape(rows_all, pair) * weight).T)
    two = dot(jnp.concatenate([sh, sl], 0), th[...].reshape(rows_all, slots))
    far_part = two[:pair] + two[pair:] + dot(sh, tl[...].reshape(rows_all, slots))
    act_mate.wait_recv()
    mine, other = so[p], sr[...]
    first = jnp.where(p == 0, mine, other)
    second = jnp.where(p == 0, other, mine)
    upd[...] = live * (fm + jnp.concatenate([first, second], 1) + far_part[:panel])
    ret_mates[1].wait_recv()
    part = cmask + far_part[panel:] + jnp.concatenate([wo[1, b] + rw[1, b] for b in range(BLK_DEV)], 1)
    ret_up.wait_recv()
    ret_dn.wait_recv()
    grad[...] = live * (part + jnp.concatenate([hb[0, b] + hb[1, b] for b in range(BLK_DEV)], 1))

    for c in (pos_up, pos_dn, feat_up, feat_dn, feat_mate, fwd_lo, fwd_hi, filt_mate, cot_mate,
              act_mate, *ret_mates.values(), ret_up, ret_dn, *sum(pre_copies, []), *sum(up_copies, [])):
        c.wait_send()

    def drain(k, carry):
        reduce_copy(k).wait_send()
        gather_copy(k).wait_send()
        return carry

    lax.fori_loop(1, n, drain, 0)


def finish(upd_in, grad_in, upd, grad):
    upd[...] = upd_in[...]
    grad[...] = grad_in[...]


def shards(n, chans, features, positions, counts, neighbours, wavevectors, filters, cotangent):
    panel, slots = features.shape
    cap = slots // BLK_DEV
    pair = 2 * panel
    groups = chans // 2
    piece = -(-(-(-2 * HALF // n)) // 32) * 32
    part_i = cap // PARTS
    vm = pltpu.VMEM
    sm = pltpu.SMEM
    scratch = [
        vm(features.shape, f32),
        vm(positions.shape, f32),
        sm(counts.shape, jnp.int32),
        sm(neighbours.shape, jnp.int32),
        vm(wavevectors.shape, jnp.int32),
        vm(filters.shape, f32),
        vm(cotangent.shape, f32),
        vm((3, 2, panel, slots), f32),
        vm((3, BLK_DEV, 8, cap), f32),
        vm((cap, 8), f32),
        vm(filters.shape, f32),
        vm((NRAD * pair, groups * pair), bf16),
        vm((NRAD * pair, groups * pair), bf16),
        vm((BLK_DEV, panel, cap), f32),
        vm((2, panel, cap), f32),
        vm((PARTS, NRAD * part_i, NB * cap), bf16),
        vm((PARTS, NRAD * part_i, NB * cap), bf16),
        vm((NB * cap, 2 * pair), bf16),
        vm((3 * BLK_DEV, cap, 2 * pair), bf16),
        vm((slots, 2 * pair), bf16),
        vm((n, piece, slots), bf16),
        vm((n, piece, slots), bf16),
        vm((n, piece, pair), f32),
        vm((n, piece, pair), f32),
        vm((n, piece, pair), f32),
        vm((PARTS, groups, part_i, pair), f32),
        vm((PARTS, max(groups - 1, 1), part_i, pair), f32),
        vm((PARTS, groups, pair, part_i), f32),
        vm((2, panel, cap), f32),
        vm((panel, cap), f32),
        vm((pair, NB * cap), f32),
        vm((3, BLK_DEV, panel, cap), f32),
        vm((3, BLK_DEV, panel, cap), f32),
        vm((3, BLK_DEV, panel, cap), f32),
        vm((2, BLK_DEV, panel, cap), f32),
        vm((2, BLK_DEV, panel, cap), f32),
        pltpu.SemaphoreType.DMA((7,)),
        pltpu.SemaphoreType.DMA((16 + 2 * PARTS * groups,)),
        pltpu.SemaphoreType.DMA((16 + 2 * PARTS * groups,)),
        pltpu.SemaphoreType.DMA((n,)),
        pltpu.SemaphoreType.DMA((n,)),
        pltpu.SemaphoreType.DMA((n,)),
        pltpu.SemaphoreType.DMA((n,)),
    ]
    whole = pl.BlockSpec(memory_space=pltpu.VMEM)
    anywhere = pl.BlockSpec(memory_space=pl.ANY)
    out = jax.ShapeDtypeStruct((panel, slots), f32)
    results = pl.pallas_call(
        functools.partial(kernel, n, chans),
        out_shape=(out, out),
        in_specs=[anywhere] * 7,
        out_specs=(whole, whole),
        scratch_shapes=scratch,
        compiler_params=pltpu.CompilerParams(
            collective_id=0, has_side_effects=True, vmem_limit_bytes=60 * 1024 * 1024),
    )(features, positions, counts, neighbours, wavevectors, filters, cotangent)
    return pl.pallas_call(
        finish,
        out_shape=(out, out),
        in_specs=[whole, whole],
        out_specs=(whole, whole),
        compiler_params=pltpu.CompilerParams(vmem_limit_bytes=60 * 1024 * 1024),
    )(*results)


def solution(mesh):
    return jax.shard_map(
        functools.partial(shards, mesh.shape["space"], mesh.shape["chan"]),
        mesh=mesh,
        in_specs=(
            P("chan", "space"),
            P(None, "space"),
            P("space"),
            P("space", None),
            P(),
            P(None, "chan", None),
            P("chan", "space"),
        ),
        out_specs=(P("chan", "space"), P("chan", "space")),
        check_vma=False,
    )
```

```python
import functools
import math

import jax
import jax.numpy as jnp
from jax import lax
from jax.experimental import pallas as pl
from jax.experimental.pallas import tpu as pltpu
from jax.sharding import PartitionSpec as P

NRAD = 8
NB = 4
BLK_DEV = 2
PARTS = 2
MOST = 4
SIDE = 2 * MOST + 1
HALF = (SIDE**3 - 1) // 2
MESH = pl.DeviceIdType.MESH
f32 = jnp.float32
bf16 = jnp.bfloat16


def halves(x):
    high = x.astype(bf16)
    return high, (x - high.astype(f32)).astype(bf16)


def dot(a, b):
    return jnp.dot(a, b, preferred_element_type=f32)


def turn_cos_sin(p):
    r = (p - jnp.floor(p + 0.5)) * math.pi
    s2 = r * r
    s = 1.0 / 6227020800.0
    for n in (-1.0 / 39916800.0, 1.0 / 362880.0, -1.0 / 5040.0, 1.0 / 120.0, -1.0 / 6.0, 1.0):
        s = s * s2 + n
    s = s * r
    c = 1.0 / 479001600.0
    for n in (-1.0 / 3628800.0, 1.0 / 40320.0, -1.0 / 720.0, 1.0 / 24.0, -0.5, 1.0):
        c = c * s2 + n
    return 1.0 - 2.0 * s * s, 2.0 * s * c


def lattice(first, rows):
    f = lax.broadcasted_iota(jnp.int32, (rows, 1), 0).astype(f32) + (first + HALF + 1.0)
    a = jnp.floor((f + 0.5) * (1.0 / (SIDE * SIDE)))
    rest = f - a * (SIDE * SIDE)
    b = jnp.floor((rest + 0.5) * (1.0 / SIDE))
    c = rest - b * SIDE
    return f, a - MOST, b - MOST, c - MOST


def kernel(n, chans, feat_in, pos_in, counts_in, nbr_in, wv_in, filt_in, cot_in, upd, grad, live_out,
           feat, pos, counts, nbr, wv, filt, cot,
           f6, p6, pt, fx, fh, fl, cm, c2, gh, gl, mts, mt, vs, th, tl, ss, rb, sg, ps, rx, ug, so, sr,
           re, wo, wp, rw, rt, hb, load_s, misc_s, misc_r, red_s, red_r, gat_s, gat_r):
    loads = [
        pltpu.make_async_copy(a, b, load_s.at[i])
        for i, (a, b) in enumerate(zip(
            (feat_in, pos_in, counts_in, nbr_in, wv_in, filt_in, cot_in),
            (feat, pos, counts, nbr, wv, filt, cot)))
    ]
    for c in loads:
        c.start()
    panel, slots = feat.shape
    cap = slots // BLK_DEV
    piece = ss.shape[1]
    grain = piece // 2
    rows_all = n * piece
    pair = 2 * panel
    groups = chans // 2
    s = lax.axis_index("space")
    q = lax.axis_index("chan")
    p = lax.rem(q, 2)
    h = lax.div(q, 2)
    mate = (s, q + 1 - 2 * p)
    nxt = (lax.rem(s + 1, n), q)
    prv = (lax.rem(s + n - 1, n), q)

    def remote(src, dst, at, dev):
        return pltpu.make_async_remote_copy(
            src_ref=src, dst_ref=dst, send_sem=misc_s.at[at], recv_sem=misc_r.at[at],
            device_id=dev, device_id_type=MESH)

    barrier = pltpu.get_barrier_semaphore()

    def greet(k, carry):
        pl.semaphore_signal(barrier, inc=1, device_id=(lax.rem(s + k, n), q), device_id_type=MESH)
        return carry

    lax.fori_loop(1, n, greet, 0)
    pl.semaphore_signal(barrier, inc=1, device_id=mate, device_id_type=MESH)
    for k in range(1, groups):
        pl.semaphore_signal(barrier, inc=1, device_id=(s, lax.rem(q + 2 * k, chans)), device_id_type=MESH)

    for at in (0, 1, 2, 6):
        loads[at].wait()
    lane = lax.broadcasted_iota(jnp.int32, (1, slots), 1)
    bound = jnp.where(lane < cap, counts[0], counts[1] + cap)
    live = (lane < bound).astype(f32)
    fm = feat[...] * live
    cmask = cot[...] * live
    f6[1, 0] = fm
    for b in range(BLK_DEV):
        cm[b] = cmask[:, b * cap:(b + 1) * cap]
    p6[1] = jnp.zeros(p6.shape[1:], f32)
    for b in range(BLK_DEV):
        p6[1, b, 0:3, :] = pos[:, b * cap:(b + 1) * cap]

    def split_filters(src, i):
        for r in range(NRAD):
            a, b = halves(src[r] * math.exp(-0.5 * r * r))
            at = r * pair + i * panel
            fh[at:at + panel, :] = a
            fl[at:at + panel, :] = b

    loads[5].wait()
    split_filters(filt, 0)
    loads[4].wait()
    f, a, b, c = lattice(0.0, n * grain)
    wf = wv[...].astype(f32) + MOST
    key = (wf[0:1] * SIDE + wf[1:2]) * SIDE + wf[2:3]
    hit = (key == f).astype(f32) + ((2.0 * HALF - key) == f).astype(f32)
    times = jnp.sum(hit, axis=1, keepdims=True)
    qa = a * (2.0 * math.pi / n)
    qb = b * (2.0 * math.pi / BLK_DEV)
    qc = c * (2.0 * math.pi)
    k2 = qa * qa + qb * qb + qc * qc
    raw = jnp.exp(-k2 / 2000.0) / (k2 + 100.0)
    norm = jnp.sum(times * raw * raw, axis=0, keepdims=True)
    weight = times * raw * lax.rsqrt(norm) * math.sqrt(3.0 / (n * slots))
    weight = weight.reshape(n, grain, 1)
    weight = jnp.concatenate([weight, weight], 1).reshape(rows_all, 1)

    pl.semaphore_wait(barrier, n - 1 + 1 + groups - 1)

    pos_up = remote(p6.at[1], p6.at[0], 0, nxt)
    pos_dn = remote(p6.at[1], p6.at[2], 1, prv)
    feat_up = remote(f6.at[1, 0], f6.at[0, 0], 2, nxt)
    feat_dn = remote(f6.at[1, 0], f6.at[2, 0], 3, prv)
    feat_mate = remote(f6.at[1, 0], f6.at[1, 1], 4, mate)
    fwd_lo = remote(f6.at[0, 0], f6.at[0, 1], 5, mate)
    fwd_hi = remote(f6.at[2, 0], f6.at[2, 1], 6, mate)
    filt_mate = remote(filt_in, fx, 7, mate)
    cot_mate = remote(cm.at[1 - p], c2.at[p], 8, mate)
    for c in (pos_up, pos_dn, feat_up, feat_dn, feat_mate, filt_mate, cot_mate):
        c.start()
    c2[p] = cm[p]

    chunk = 16
    layer_x = s.astype(f32)
    xs = (pos[0:1, :] + layer_x) * (1.0 / n)
    ys = pos[1:2, :] * (1.0 / BLK_DEV)
    zs = pos[2:3, :]

    def reduce_copy(k):
        return pltpu.make_async_remote_copy(
            src_ref=ss.at[lax.rem(s + k, n)], dst_ref=rb.at[s], send_sem=red_s.at[k],
            recv_sem=red_r.at[k], device_id=(lax.rem(s + k, n), q), device_id_type=MESH)

    vs[...] = jnp.concatenate(halves(jnp.concatenate([fm, cmask], 0).T), 1)

    def piece_sums(to, carry):
        for at in range(0, grain, chunk):
            _, a, b, c = lattice((to * grain + at).astype(f32), chunk)
            cosv, sinv = turn_cos_sin(a * xs + b * ys + c * zs)
            th[to, at:at + chunk, :], tl[to, at:at + chunk, :] = halves(cosv)
            th[to, grain + at:grain + at + chunk, :], tl[to, grain + at:grain + at + chunk, :] = halves(sinv)
        two = dot(th[to], vs[...])
        ss[to] = two[:, :pair] + two[:, pair:] + dot(tl[to], vs[:, :pair])
        return carry

    lax.fori_loop(0, n, piece_sums, 0)

    def start_reduce(k, carry):
        reduce_copy(k).start()
        return carry

    pos_up.wait_recv()
    pos_dn.wait_recv()
    pt[...] = p6[1, p].T
    loads[3].wait()
    step = 16
    part_i = cap // PARTS
    chosen = [nbr[p, e] for e in range(NB)]

    for half in range(PARTS):
        def radial(i, carry):
            at = pl.multiple_of(i * step, step)
            own = pt[pl.ds(half * part_i + at, step), :]
            for e in range(NB):
                w = chosen[e]
                far = p6[lax.div(w, BLK_DEV), lax.rem(w, BLK_DEV)]
                offset = (lax.div(w, BLK_DEV) - 1).astype(f32)
                dx = own[:, 0:1] - (far[0:1, :] + offset)
                dy = own[:, 1:2] - far[1:2, :]
                dz = own[:, 2:3] - far[2:3, :]
                sq = jnp.minimum(dx * dx + dy * dy + dz * dz, 1.0)
                left = 1.0 - sq
                u = NRAD * jnp.sqrt(sq) - 0.5
                t = jnp.exp(u)
                g = jnp.exp(-0.5 * u * u) * (0.3 * left * left)
                for r in range(NRAD):
                    if r:
                        g = g * t
                    a, b = halves(g)
                    gh[half, pl.ds(r * part_i + at, step), e * cap:(e + 1) * cap] = a
                    gl[half, pl.ds(r * part_i + at, step), e * cap:(e + 1) * cap] = b
            return carry

        lax.fori_loop(0, part_i // step, radial, 0)
        if half == 0:
            feat_up.wait_recv()
            fwd_lo.start()
            feat_dn.wait_recv()
            fwd_hi.start()
            lax.fori_loop(1, n, start_reduce, 0)

    filt_mate.wait_recv()
    split_filters(fx, 1)

    feat_mate.wait_recv()
    fwd_lo.wait_recv()
    fwd_hi.wait_recv()
    for layer in range(3):
        both = jnp.concatenate([f6[layer, 0], f6[layer, 1]], 0)
        for b in range(BLK_DEV):
            a, c = halves(both[:, b * cap:(b + 1) * cap].T)
            mt[layer * BLK_DEV + b] = jnp.concatenate([a, c], 1)
    for e in range(NB):
        mts[e * cap:(e + 1) * cap, :] = mt[chosen[e]]
    def gather_copy(k):
        return pltpu.make_async_remote_copy(
            src_ref=sg.at[s], dst_ref=sg.at[s], send_sem=gat_s.at[k],
            recv_sem=gat_r.at[k], device_id=(lax.rem(s + k, n), q), device_id_type=MESH)

    def all_gather_start():
        def wait_reduce(k, carry):
            reduce_copy(k).wait_recv()
            return carry

        lax.fori_loop(1, n, wait_reduce, 0)
        rb[s] = ss[s]

        def add_up(k, acc):
            return acc + rb[k]

        sg[s] = lax.fori_loop(0, n, add_up, jnp.zeros((piece, pair), f32))

        def start_gather(k, carry):
            gather_copy(k).start()
            return carry

        lax.fori_loop(1, n, start_gather, 0)

    pre_copies = []
    for half in range(PARTS):
        two = dot(gh[half], mts[...])
        sums = two[:, :pair] + two[:, pair:] + dot(gl[half], mts[:, :pair])
        a, b = halves(sums)
        a = jnp.concatenate([a[r * part_i:(r + 1) * part_i] for r in range(NRAD)], 1)
        b = jnp.concatenate([b[r * part_i:(r + 1) * part_i] for r in range(NRAD)], 1)
        two = dot(jnp.concatenate([a, b], 0), fh[...])
        total = two[:part_i] + two[part_i:] + dot(a, fl[...])
        for k in range(groups):
            ps[half, k] = total[:, k * pair:(k + 1) * pair]
        copies = []
        for k in range(1, groups):
            c = remote(ps.at[half, lax.rem(h + k, groups)], rx.at[half, k - 1], 16 + half * groups + k,
                       (s, lax.rem(q + 2 * k, chans)))
            c.start()
            copies.append(c)
        pre_copies.append(copies)

    cot_mate.wait_recv()
    up_copies = []
    for half in range(PARTS):
        here = slice(half * part_i, (half + 1) * part_i)
        for c in pre_copies[half]:
            c.wait_recv()
        acc = ps[half, h]
        for k in range(1, groups):
            acc = acc + rx[half, k - 1]
        pre = acc.T
        sigma = 1.0 / (1.0 + jnp.exp(-pre))
        act = pre * sigma
        ug[half, h] = jnp.concatenate([c2[0, :, here], c2[1, :, here]], 0) * sigma * (1.0 + pre * (1.0 - sigma))
        copies = []
        for k in range(1, groups):
            c = pltpu.make_async_remote_copy(
                src_ref=ug.at[half, h], dst_ref=ug.at[half, h], send_sem=misc_s.at[16 + (PARTS + half) * groups + k],
                recv_sem=misc_r.at[16 + (PARTS + half) * groups + k],
                device_id=(s, lax.rem(q + 2 * k, chans)), device_id_type=MESH)
            c.start()
            copies.append(c)
        up_copies.append(copies)
        so[0, :, here] = act[:panel]
        so[1, :, here] = act[panel:]
        if half == 0:
            all_gather_start()
    act_mate = remote(so.at[1 - p], sr, 9, mate)
    act_mate.start()

    pair_cots = []
    for half in range(PARTS):
        for c in up_copies[half]:
            c.wait_recv()
        uh, ul = halves(ug[half].reshape(groups * pair, part_i))
        two = dot(fh[...], jnp.concatenate([uh, ul], 1))
        a, b = halves(two[:, :part_i] + two[:, part_i:] + dot(fl[...], uh))
        a = jnp.concatenate([a[r * pair:(r + 1) * pair] for r in range(NRAD)], 1)
        b = jnp.concatenate([b[r * pair:(r + 1) * pair] for r in range(NRAD)], 1)
        both = jnp.concatenate([a, b], 0)
        pair_cots.append((a, both))
        out = dot(both, gh[half, :, cap:])
        out = out[:pair] + out[pair:] + dot(a, gl[half, :, cap:])
        if half == 0:
            re[:, cap:] = out
        else:
            re[:, cap:] += out
    ret_mates = {}

    def window_sums(layer, entries):
        for blk in range(BLK_DEV):
            w = layer * BLK_DEV + blk
            acc = None
            for e in entries:
                term = jnp.where(chosen[e] == w, re[:, e * cap:(e + 1) * cap], 0.0)
                acc = term if acc is None else acc + term
            wo[layer, blk] = acc[:panel]
            wp[layer, blk] = acc[panel:]
        ret_mates[layer] = remote(wp.at[layer], rw.at[layer], 10 + layer, mate)
        ret_mates[layer].start()

    window_sums(0, range(1, NB))
    window_sums(2, range(1, NB))
    out = None
    for half in range(PARTS):
        a, both = pair_cots[half]
        term = dot(both, gh[half, :, :cap])
        term = term[:pair] + term[pair:] + dot(a, gl[half, :, :cap])
        out = term if half == 0 else out + term
    re[:, :cap] = out
    ret_up = remote(rt.at[1], hb.at[0], 13, nxt)
    ret_dn = remote(rt.at[0], hb.at[1], 14, prv)
    ret_mates[0].wait_recv()
    rt[0] = wo[0] + rw[0]
    ret_dn.start()
    ret_mates[2].wait_recv()
    rt[1] = wo[2] + rw[2]
    ret_up.start()
    window_sums(1, range(NB))

    def wait_gather(k, carry):
        gather_copy(k).wait_recv()
        return carry

    lax.fori_loop(1, n, wait_gather, 0)
    sh, sl = halves((sg[...].reshape(rows_all, pair) * weight).T)
    two = dot(jnp.concatenate([sh, sl], 0), th[...].reshape(rows_all, slots))
    far_part = two[:pair] + two[pair:] + dot(sh, tl[...].reshape(rows_all, slots))
    act_mate.wait_recv()
    mine, other = so[p], sr[...]
    first = jnp.where(p == 0, mine, other)
    second = jnp.where(p == 0, other, mine)
    live_out[...] = jnp.broadcast_to(live, live_out.shape)
    upd[...] = (fm + jnp.concatenate([first, second], 1) + far_part[:panel])
    ret_mates[1].wait_recv()
    part = cmask + far_part[panel:] + jnp.concatenate([wo[1, b] + rw[1, b] for b in range(BLK_DEV)], 1)
    ret_up.wait_recv()
    ret_dn.wait_recv()
    grad[...] = (part + jnp.concatenate([hb[0, b] + hb[1, b] for b in range(BLK_DEV)], 1))

    for c in (pos_up, pos_dn, feat_up, feat_dn, feat_mate, fwd_lo, fwd_hi, filt_mate, cot_mate,
              act_mate, *ret_mates.values(), ret_up, ret_dn, *sum(pre_copies, []), *sum(up_copies, [])):
        c.wait_send()

    def drain(k, carry):
        reduce_copy(k).wait_send()
        gather_copy(k).wait_send()
        return carry

    lax.fori_loop(1, n, drain, 0)


def shards(n, chans, features, positions, counts, neighbours, wavevectors, filters, cotangent):
    panel, slots = features.shape
    cap = slots // BLK_DEV
    pair = 2 * panel
    groups = chans // 2
    piece = -(-(-(-2 * HALF // n)) // 32) * 32
    part_i = cap // PARTS
    vm = pltpu.VMEM
    sm = pltpu.SMEM
    scratch = [
        vm(features.shape, f32),
        vm(positions.shape, f32),
        sm(counts.shape, jnp.int32),
        sm(neighbours.shape, jnp.int32),
        vm(wavevectors.shape, jnp.int32),
        vm(filters.shape, f32),
        vm(cotangent.shape, f32),
        vm((3, 2, panel, slots), f32),
        vm((3, BLK_DEV, 8, cap), f32),
        vm((cap, 8), f32),
        vm(filters.shape, f32),
        vm((NRAD * pair, groups * pair), bf16),
        vm((NRAD * pair, groups * pair), bf16),
        vm((BLK_DEV, panel, cap), f32),
        vm((2, panel, cap), f32),
        vm((PARTS, NRAD * part_i, NB * cap), bf16),
        vm((PARTS, NRAD * part_i, NB * cap), bf16),
        vm((NB * cap, 2 * pair), bf16),
        vm((3 * BLK_DEV, cap, 2 * pair), bf16),
        vm((slots, 2 * pair), bf16),
        vm((n, piece, slots), bf16),
        vm((n, piece, slots), bf16),
        vm((n, piece, pair), f32),
        vm((n, piece, pair), f32),
        vm((n, piece, pair), f32),
        vm((PARTS, groups, part_i, pair), f32),
        vm((PARTS, max(groups - 1, 1), part_i, pair), f32),
        vm((PARTS, groups, pair, part_i), f32),
        vm((2, panel, cap), f32),
        vm((panel, cap), f32),
        vm((pair, NB * cap), f32),
        vm((3, BLK_DEV, panel, cap), f32),
        vm((3, BLK_DEV, panel, cap), f32),
        vm((3, BLK_DEV, panel, cap), f32),
        vm((2, BLK_DEV, panel, cap), f32),
        vm((2, BLK_DEV, panel, cap), f32),
        pltpu.SemaphoreType.DMA((7,)),
        pltpu.SemaphoreType.DMA((16 + 2 * PARTS * groups,)),
        pltpu.SemaphoreType.DMA((16 + 2 * PARTS * groups,)),
        pltpu.SemaphoreType.DMA((n,)),
        pltpu.SemaphoreType.DMA((n,)),
        pltpu.SemaphoreType.DMA((n,)),
        pltpu.SemaphoreType.DMA((n,)),
    ]
    whole = pl.BlockSpec(memory_space=pltpu.VMEM)
    anywhere = pl.BlockSpec(memory_space=pl.ANY)
    out = jax.ShapeDtypeStruct((panel, slots), f32)
    upd, grad, live = pl.pallas_call(
        functools.partial(kernel, n, chans),
        out_shape=(out, out, out),
        in_specs=[anywhere] * 7,
        out_specs=(whole, whole, whole),
        scratch_shapes=scratch,
        compiler_params=pltpu.CompilerParams(
            collective_id=0, has_side_effects=True, vmem_limit_bytes=60 * 1024 * 1024),
    )(features, positions, counts, neighbours, wavevectors, filters, cotangent)
    return upd * live, grad * live


def solution(mesh):
    return jax.shard_map(
        functools.partial(shards, mesh.shape["space"], mesh.shape["chan"]),
        mesh=mesh,
        in_specs=(
            P("chan", "space"),
            P(None, "space"),
            P("space"),
            P("space", None),
            P(),
            P(None, "chan", None),
            P("chan", "space"),
        ),
        out_specs=(P("chan", "space"), P("chan", "space")),
        check_vma=False,
    )
```
